128 devices in a mesh: mem: 4 (over z), var: 32 (over y, x, core).
Axes of the slice: x: 4, y: 4, z: 4, core: 2. Of those that a mesh axis runs over, the one named last changes fastest.
Arguments:
- prior_state: float32 [256, 262144], P(('mem', 'var')), may hold values from -6 to 6
- obs_value: float32 [2, 1024], replicated, may hold values from -6 to 6
- obs_error: float32 [2, 1024], replicated, may hold values from 0.5 to 2
- obs_owner: int32 [2, 1024], replicated, may hold values from 0 to 127, as said below
- obs_offset: int32 [2, 1024], replicated, may hold values from 0 to 2047
- taper_table: float32 [64], replicated, may hold values from 0 to 1.3, as said below
Outputs:
- posterior_state: float32 [256, 262144], P(('mem', 'var'))
The draws below stay inside these ranges and needn't reach their ends.
Inputs may be any that keep to these rules, and one draw needn't show every extreme that they name: `taper_table`: the weights follow the Gaspari-Cohn shape over the bins, each bin scaled by its own factor; the last bin is zero. `obs_owner`: in each block every owner holds exactly 8 observations.
All inputs are finite; a program needn't handle non-finite values.
Results may differ from the reference program's by a relative error of at most 0.0003.
Values sent between devices are 32-bit elements; how exact they have to be, the bound alone decides.
No kernel may reach another device: no remote copies, remote signals or barrier semaphores. Data moves between devices by JAX's collectives and lax.ppermute only.
A program may use at most 64 MiB of HBM per device.

```python
import math
import jax
import jax.numpy as jnp
from jax import lax

MEMBERS = 256
NV_DEV = 2048
NOBS = 1024
BLOCKS = 2
NBINS = 64
NV = 262144
BIN_WIDTH = 4096
DEVICES = 128


def draw_taper_table(key, part):
    key = jax.random.fold_in(key, 7)
    steps = jnp.arange(NBINS, dtype=jnp.float32)
    ratio = steps * 2.0 / (NBINS - 1)
    safe = jnp.maximum(ratio, 1.0)
    inner = -0.25 * ratio ** 5 + 0.5 * ratio ** 4 + 0.625 * ratio ** 3 - 5.0 / 3.0 * ratio ** 2 + 1.0
    outer = ratio ** 5 / 12.0 - 0.5 * ratio ** 4 + 0.625 * ratio ** 3 + 5.0 / 3.0 * ratio ** 2 - 5.0 * ratio + 4.0 - 2.0 / (3.0 * safe)
    shape = jnp.where(ratio <= 1.0, inner, outer)
    shape = jnp.clip(shape, 0.0, 1.0)
    factor = jax.random.uniform(key, (NBINS,), jnp.float32, 0.7, 1.3)
    return jnp.where(steps >= NBINS - 1, 0.0, shape * factor).astype(jnp.float32)


def draw_obs_owner(key, part):
    key = jax.random.fold_in(key, 11)
    per_owner = NOBS // DEVICES
    rows = []
    for block in range(BLOCKS):
        order = jax.random.permutation(jax.random.fold_in(key, block), NOBS)
        rows.append((order // per_owner).astype(jnp.int32))
    return jnp.stack(rows, axis=0).astype(jnp.int32)


def with_ends(drawn, rng, least, top_value):
    dims = drawn.shape
    spot = [jax.random.randint(jax.random.fold_in(rng, axis), (), 0, dims[axis]) for axis in range(len(dims))]
    drawn = drawn.at[tuple(spot)].set(least)
    longest = dims.index(max(dims))
    spot[longest] = (spot[longest] + 1) % dims[longest]
    return drawn.at[tuple(spot)].set(top_value)


def levels(stream_key, extent, cuts, least, high):
    level = 1.0
    for position, parts in cuts:
        draws = jax.random.uniform(jax.random.fold_in(jax.random.fold_in(stream_key, 6), position), (parts,), jnp.float32, least / len(cuts), high / len(cuts))
        level = level * jnp.repeat(jnp.exp(draws), extent[position] // parts).reshape((-1,) + (1,) * (len(extent) - 1 - position))
    return level


def bell_draw(stream_key, shape, scale, bound, cuts=(), kind=jnp.bfloat16):
    result = scale * jax.random.normal(stream_key, shape, jnp.float32)
    if cuts:
        result = result * levels(stream_key, shape, cuts, -0.22, 0.18)
    return jnp.clip(result, -bound, bound).astype(kind)


def setup_inputs(seed: int = 0) -> dict:
    seeds = jax.random.split(jax.random.key(seed), 7)
    prior_state = bell_draw(seeds[0], (MEMBERS, NV), 1.0, 6.0, ((0, 128),), jnp.float32)
    obs_value = bell_draw(seeds[1], (BLOCKS, NOBS), 1.0, 6.0, (), jnp.float32)
    obs_error = jnp.clip(jnp.exp(jax.random.uniform(seeds[2], (BLOCKS, NOBS), jnp.float32, math.log(0.5), math.log(2.0))), 0.5, 2.0)
    obs_owner = draw_obs_owner(jax.random.fold_in(seeds[6], 71), 0)
    obs_offset = with_ends(jax.random.randint(seeds[4], (BLOCKS, NOBS), 0, NV_DEV), jax.random.fold_in(seeds[4], 1), 0, NV_DEV - 1).astype(jnp.int32)
    taper_table = draw_taper_table(jax.random.fold_in(seeds[6], 71), 0)
    return dict(prior_state=prior_state, obs_value=obs_value, obs_error=obs_error, obs_owner=obs_owner, obs_offset=obs_offset, taper_table=taper_table)


def increments(prior, value, error):
    mean = lax.optimization_barrier(jnp.mean(prior, axis=1, keepdims=True))
    anom = prior - mean
    varian = lax.optimization_barrier(jnp.sum(anom * anom, axis=1)) / (MEMBERS - 1) + 1e-06
    noise = error[:, None]
    spread = varian[:, None]
    post_mean = (noise * mean + spread * value[:, None]) / (spread + noise)
    shrink = jnp.sqrt(noise / (spread + noise))
    return (anom, varian, post_mean + shrink * anom - prior)

def update_block(states, start, anom, varian, change, obs_pos, taper_table):
    width = states.shape[1]
    centred = states - lax.optimization_barrier(jnp.mean(states, axis=0, keepdims=True))
    cov = jnp.dot(anom, centred, precision=lax.Precision.HIGHEST, preferred_element_type=jnp.float32) / (MEMBERS - 1)
    places = start + jnp.arange(width, dtype=jnp.int32)
    dist = jnp.abs(places[None, :] - obs_pos[:, None])
    bins = jnp.minimum(dist // BIN_WIDTH, NBINS - 1)
    gain = jnp.take(taper_table, bins) * cov / varian[:, None]
    return states + jnp.dot(change.T, gain, precision=lax.Precision.HIGHEST, preferred_element_type=jnp.float32)

def reference(prior_state, obs_value, obs_error, obs_owner, obs_offset, taper_table):
    count = NV // NV_DEV
    state = prior_state
    for block in range(BLOCKS):
        obs_pos = (obs_owner[block] * NV_DEV + obs_offset[block]).astype(jnp.int32)
        prior = jnp.take(state, obs_pos, axis=1).T
        anom, varian, change = increments(prior, obs_value[block], obs_error[block])
        pieces = state.reshape(MEMBERS, count, NV_DEV).transpose(1, 0, 2)
        starts = jnp.arange(count, dtype=jnp.int32) * NV_DEV

        def one(item):
            return update_block(item[0], item[1], anom, varian, change, obs_pos, taper_table)
        pieces = lax.map(one, (pieces, starts))
        state = pieces.transpose(1, 0, 2).reshape(MEMBERS, NV)
    return state
```

```python
import functools

import jax
import jax.numpy as jnp
from jax import lax
from jax.experimental import pallas as pl
from jax.experimental.layout import Layout, with_layout_constraint
from jax.experimental.pallas import tpu as pltpu
from jax.sharding import PartitionSpec as P

MEMBERS = 256
NDEV = 128
NOBS = 1024
HALF = NOBS // 2
NV_DEV = 2048
LANES = 128
TILES = NV_DEV // LANES
STATE_ROWS = 2 * TILES
OBS_ROWS = 32
MSG = STATE_ROWS + OBS_ROWS
WIDE = 256
F32 = jnp.float32
BF16 = jnp.bfloat16


def iota(shape, dim):
    return lax.broadcasted_iota(jnp.int32, shape, dim)


def split(x):
    hi = x.astype(BF16)
    return hi, (x - hi.astype(F32)).astype(BF16)


def dot3(a, b, dims=(((1,), (0,)), ((), ()))):
    ca, cb = dims[0][0][0], dims[0][1][0]
    left = jnp.concatenate([a[0], a[1], a[0]], axis=ca)
    right = jnp.concatenate([b[0], b[0], b[1]], axis=cb)
    return lax.dot_general(left, right, dims, preferred_element_type=F32)


def by_parity(x):
    lane = iota((4, LANES), 1)
    first, second = x[0:4], x[4:8]
    even = jnp.where(lane < 64, first, pltpu.roll(second, 64, 1))
    odd = jnp.where(lane < 64, pltpu.roll(first, 64, 1), second)
    return even, odd


def prep_kernel(me_ref, owner_ref, offset_ref, value_ref, error_ref, state_ref, msg_ref, field_ref):
    odd_device = me_ref[0] % 2 == 1
    row = iota((LANES, LANES), 0)
    row_owner = (2 * row) % LANES + row // 64
    before = jnp.where(row < iota((LANES, LANES), 1), 1.0, 0.0).astype(BF16)
    slot = iota((8, NOBS), 0).astype(F32)
    tables = []
    for b in range(2):
        hot = []
        ranks = []
        count = jnp.zeros((LANES, 1), F32)
        for t in range(NOBS // LANES):
            own = owner_ref[b : b + 1, t * LANES : (t + 1) * LANES]
            is_own = jnp.where(own == row_owner, 1.0, 0.0)
            ahead = jnp.dot(is_own.astype(BF16), before, preferred_element_type=F32) + count
            ranks.append(jnp.sum(is_own * ahead, axis=0, keepdims=True))
            count = count + jnp.sum(is_own, axis=1, keepdims=True)
            hot.append(is_own.astype(BF16))
        hot = jnp.concatenate(hot, axis=1)
        here = jnp.concatenate(ranks, axis=1) == slot
        off = offset_ref[b : b + 1, :]
        parts = [(off // LANES).astype(F32), (off % LANES).astype(F32)]
        for ref in (value_ref, error_ref):
            rest = ref[b : b + 1, :]
            for _ in range(3):
                part = rest.astype(BF16).astype(F32)
                parts.append(part)
                rest = rest - part
        rows = jnp.concatenate([jnp.where(here, p, 0.0).astype(BF16) for p in parts], axis=0)
        tables.append(
            lax.dot_general(rows, hot, (((1,), (1,)), ((), ())), preferred_element_type=F32)
        )
    for b in range(2):
        t = tables[b]
        off = t[0:8] * float(LANES) + t[8:16]
        val = (t[16:24] + t[24:32]) + t[32:40]
        err = (t[40:48] + t[48:56]) + t[56:64]
        for f, x in enumerate((off, val, err)):
            even, odd = by_parity(x)
            same = jnp.where(odd_device, odd, even)
            other = jnp.where(odd_device, even, odd)
            field_ref[(b * 3 + f) * 8 : (b * 3 + f) * 8 + 8, :] = jnp.concatenate([same, other], axis=0)
    pad = jnp.zeros((LANES - 16, LANES), F32)
    tile_of = jnp.concatenate([tables[0][0:8], tables[1][0:8], pad], axis=0).T.astype(jnp.int32)
    lane_of = jnp.concatenate([tables[0][8:16], tables[1][8:16], pad], axis=0).T.astype(jnp.int32)
    picked = []
    for r in range(2):
        groups = []
        for g in range(16):
            want_tile = tile_of[g * 8 : g * 8 + 8, :]
            want_lane = lane_of[g * 8 : g * 8 + 8, :]
            first = 16 * g if g < 8 else 16 * (g - 8) + 1
            acc = jnp.zeros((8, LANES), F32)
            for c in range(TILES):
                x = state_ref[pl.ds(first * STATE_ROWS + c * 2 + r, 8, stride=2 * STATE_ROWS), :]
                acc = jnp.where(want_tile == c, jnp.take_along_axis(x, want_lane, axis=1), acc)
            groups.append(acc)
        found = jnp.concatenate(groups, axis=0).T
        for b in range(2):
            even, odd = by_parity(found[b * 8 : b * 8 + 8])
            picked.extend([even, odd])
    picked = jnp.concatenate(picked, axis=0)

    def fill(d, _):
        msg_ref[pl.ds(d * MSG, STATE_ROWS), :] = state_ref[pl.ds(d * STATE_ROWS, STATE_ROWS), :]
        msg_ref[pl.ds(d * MSG + STATE_ROWS, OBS_ROWS), :] = picked
        return 0

    lax.fori_loop(0, NDEV, fill, 0, unroll=8)


def columns(row):
    return jnp.broadcast_to(row, (LANES, LANES)).T


def stats(raw, value, error):
    mean = jnp.sum(raw, axis=0, keepdims=True) * (1.0 / MEMBERS)
    anom = raw - mean
    varian = jnp.sum(anom * anom, axis=0, keepdims=True) * (1.0 / (MEMBERS - 1)) + 1e-06
    total = varian + error
    shrink = jnp.sqrt(error / total)
    scale = -1.0 / ((MEMBERS - 1) * total * (1.0 + shrink))
    push = anom - (value - mean) * (1.0 + shrink)
    return anom, anom * scale, push


def main_kernel(
    me_ref, table_ref, field_ref, recv_ref, out_ref,
    left_hi, left_lo, push_hi, push_lo, const_hi, const_lo, thr, low, high, off_col, raw2,
):
    me = me_ref[0]
    par = me % 2
    mine = me // 2
    table8 = jnp.broadcast_to(table_ref[...], (8, LANES))
    table = jnp.broadcast_to(table_ref[...], (LANES, LANES))

    def load_obs(b):
        out = []
        for which in (par, 1 - par):
            for s in range(4):
                at = STATE_ROWS + b * 8 + which * 4 + s
                out.append(
                    jnp.concatenate(
                        [recv_ref[pl.ds(at + r * 16, NDEV, stride=MSG), :] for r in range(2)], axis=0
                    )
                )
        return jnp.concatenate(out, axis=1)

    def field(b, f):
        base = (b * 3 + f) * 8
        return jnp.concatenate([field_ref[base + i : base + i + 1, :] for i in range(8)], axis=1)

    lane64 = iota((8, LANES), 1) % 64
    delta = mine - lane64
    steps = jnp.abs(delta)
    w_far = jnp.take_along_axis(table8, steps, axis=1)[0:1]
    w_near = jnp.take_along_axis(table8, jnp.maximum(steps - 1, 0), axis=1)[0:1]
    w_other = jnp.take_along_axis(table8, jnp.abs(2 * delta + 2 * par - 1) // 2, axis=1)[0:1]
    ahead = delta[0:1] > 0
    w_low = jnp.where(ahead, w_near, w_far)
    w_high = jnp.where(ahead, w_far, w_near)
    shift = jnp.where(ahead, 0.0, 1.0)
    w_other4 = jnp.concatenate([w_other] * 4, axis=1)

    def block_setup(b, raw):
        anom, scaled, push = stats(raw, field(b, 1), field(b, 2))
        hi, lo = split(scaled.T)
        left_hi[b, :, :] = hi
        left_lo[b, :, :] = lo
        ph, pw = split(push)
        push_hi[b, :, :] = ph
        push_lo[b, :, :] = pw
        weighted = split(scaled[:, HALF:] * w_other4)
        const = dot3((ph[:, HALF:], pw[:, HALF:]), weighted, (((1,), (1,)), ((), ())))
        ch, cl = split(const)
        const_hi[b, :, :] = ch
        const_lo[b, :, :] = cl
        off = field(b, 0)
        for s in range(4):
            thr[b, s * LANES : (s + 1) * LANES, :] = columns(off[:, s * LANES : (s + 1) * LANES] + shift)
        return off

    low[...] = columns(w_low)
    high[...] = columns(w_high)

    off1 = block_setup(0, load_obs(0))
    for s in range(8):
        off_col[s * LANES : (s + 1) * LANES, :] = columns(off1[:, s * LANES : (s + 1) * LANES])
    raw2[...] = load_obs(1)

    d = iota((LANES, LANES), 1) % 64 - iota((LANES, LANES), 0) % 64
    ad = jnp.abs(d)
    far = jnp.take_along_axis(table, ad, axis=1)
    near = jnp.take_along_axis(table, jnp.maximum(ad - 1, 0), axis=1)
    sign = jnp.where(d > 0, 1.0, jnp.where(d < 0, -1.0, 0.0))
    to_same = jnp.take_along_axis(table, jnp.abs(2 * d + 2 * par - 1) // 2, axis=1)
    to_other = jnp.take_along_axis(table, jnp.abs(2 * d + 1 - 2 * par) // 2, axis=1)
    off2 = field(1, 0)
    for t in range(NOBS // WIDE):
        raw = raw2[:, t * WIDE : (t + 1) * WIDE]
        centred = raw - jnp.sum(raw, axis=0, keepdims=True) * (1.0 / MEMBERS)
        cov = dot3((left_hi[0], left_lo[0]), split(centred))
        in_same = t < NOBS // WIDE // 2
        pieces = []
        for k in range(8):
            line = []
            for h in range(WIDE // LANES):
                c = cov[k * LANES : (k + 1) * LANES, h * LANES : (h + 1) * LANES]
                if (k < 4) == in_same:
                    at = t * WIDE + h * LANES
                    gap = off2[:, at : at + LANES] - off_col[k * LANES : (k + 1) * LANES, :]
                    w = jnp.where(gap * sign >= 0.0, far, near)
                else:
                    w = to_same if in_same else to_other
                line.append(c * w)
            pieces.append(jnp.concatenate(line, axis=1))
        gain = split(jnp.concatenate(pieces, axis=0))
        raw2[:, t * WIDE : (t + 1) * WIDE] = raw + dot3((push_hi[0], push_lo[0]), gain)
    block_setup(1, raw2[...])

    def tile(t, _):
        at = t * (WIDE // LANES)
        raw = jnp.concatenate(
            [
                jnp.concatenate(
                    [recv_ref[pl.ds((at + h) * 2 + r, NDEV, stride=MSG), :] for r in range(2)], axis=0
                )
                for h in range(WIDE // LANES)
            ],
            axis=1,
        )
        place = [(iota((LANES, LANES), 1) + (at + h) * LANES).astype(F32) for h in range(WIDE // LANES)]
        for b in range(2):
            centred = split(raw - jnp.sum(raw, axis=0, keepdims=True) * (1.0 / MEMBERS))
            cov = dot3((left_hi[b, 0:HALF, :], left_lo[b, 0:HALF, :]), centred)
            pieces = []
            for k in range(4):
                line = []
                for h in range(WIDE // LANES):
                    c = cov[k * LANES : (k + 1) * LANES, h * LANES : (h + 1) * LANES]
                    w = jnp.where(place[h] >= thr[b, k * LANES : (k + 1) * LANES, :], high[...], low[...])
                    line.append(c * w)
                pieces.append(jnp.concatenate(line, axis=1))
            gain = split(jnp.concatenate(pieces, axis=0))
            left = (
                jnp.concatenate([push_hi[b, :, 0:HALF], const_hi[b]], axis=1),
                jnp.concatenate([push_lo[b, :, 0:HALF], const_lo[b]], axis=1),
            )
            right = tuple(jnp.concatenate([g, c], axis=0) for g, c in zip(gain, centred))
            raw = raw + dot3(left, right)
        for h in range(WIDE // LANES):
            for r in range(2):
                out_ref[pl.ds((at + h) * 2 + r, NDEV, stride=STATE_ROWS), :] = raw[
                    r * NDEV : (r + 1) * NDEV, h * LANES : (h + 1) * LANES
                ]
        return 0

    lax.fori_loop(0, NV_DEV // WIDE, tile, 0)


VMEM = pl.BlockSpec(memory_space=pltpu.VMEM)
SMEM = pl.BlockSpec(memory_space=pltpu.SMEM)
PARAMS = pltpu.CompilerParams(vmem_limit_bytes=48 * 1024 * 1024)


def prep(me, owner, offset, value, error, state):
    return pl.pallas_call(
        prep_kernel,
        out_shape=(
            jax.ShapeDtypeStruct((NDEV * MSG, LANES), F32),
            jax.ShapeDtypeStruct((48, LANES), F32),
        ),
        in_specs=[SMEM] + [VMEM] * 5,
        out_specs=(VMEM, VMEM),
        compiler_params=PARAMS,
        name="prep",
    )(me, owner, offset, value, error, state)


def assimilate(me, table, fields, recv):
    return pl.pallas_call(
        main_kernel,
        out_shape=jax.ShapeDtypeStruct((NDEV * STATE_ROWS, LANES), F32),
        in_specs=[SMEM] + [VMEM] * 3,
        out_specs=VMEM,
        scratch_shapes=[
            pltpu.VMEM((2, NOBS, MEMBERS), BF16),
            pltpu.VMEM((2, NOBS, MEMBERS), BF16),
            pltpu.VMEM((2, MEMBERS, NOBS), BF16),
            pltpu.VMEM((2, MEMBERS, NOBS), BF16),
            pltpu.VMEM((2, MEMBERS, MEMBERS), BF16),
            pltpu.VMEM((2, MEMBERS, MEMBERS), BF16),
            pltpu.VMEM((2, HALF, LANES), F32),
            pltpu.VMEM((LANES, LANES), F32),
            pltpu.VMEM((LANES, LANES), F32),
            pltpu.VMEM((NOBS, LANES), F32),
            pltpu.VMEM((MEMBERS, NOBS), F32),
        ],
        compiler_params=PARAMS,
        name="assimilate",
    )(me, table, fields, recv)


def body(prior_state, obs_value, obs_error, obs_owner, obs_offset, taper_table):
    axes = ("mem", "var")
    me = lax.axis_index(axes).astype(jnp.int32).reshape(1)
    table = jnp.pad(taper_table, (0, LANES - taper_table.shape[0])).reshape(1, LANES)
    rows = prior_state.reshape(2, NDEV * TILES, LANES).transpose(1, 0, 2).reshape(NDEV * STATE_ROWS, LANES)
    msg, fields = prep(me, obs_owner, obs_offset, obs_value, obs_error, rows)
    recv = lax.all_to_all(msg.reshape(NDEV, MSG, LANES), axes, split_axis=0, concat_axis=0, tiled=True)
    new = assimilate(me, table, fields, recv.reshape(NDEV * MSG, LANES))
    back = lax.all_to_all(
        new.reshape(NDEV, STATE_ROWS, LANES), axes, split_axis=0, concat_axis=0, tiled=True
    )
    rows = back.reshape(NDEV * TILES, 2, LANES).transpose(1, 0, 2)
    rows = with_layout_constraint(rows, Layout(major_to_minor=(1, 0, 2)))
    return rows.reshape(2, NDEV * NV_DEV)


def solution(mesh):
    in_specs = (P(("mem", "var"), None), P(), P(), P(), P(), P())
    out_specs = P(("mem", "var"), None)
    return jax.shard_map(body, mesh=mesh, in_specs=in_specs, out_specs=out_specs, check_vma=False)
```

```python
import functools

import jax
import jax.numpy as jnp
from jax import lax
from jax.experimental import pallas as pl
from jax.experimental.layout import Layout, with_layout_constraint
from jax.experimental.pallas import tpu as pltpu
from jax.sharding import PartitionSpec as P

MEMBERS = 256
NDEV = 128
NOBS = 1024
HALF = NOBS // 2
NV_DEV = 2048
LANES = 128
TILES = NV_DEV // LANES
STATE_ROWS = 2 * TILES
OBS_ROWS = 16
MSG = STATE_ROWS + OBS_ROWS
WIDE = 1024
OBS_WIDE = 512
F32 = jnp.float32
BF16 = jnp.bfloat16
VMEM_MIB = 32


def iota(shape, dim):
    return lax.broadcasted_iota(jnp.int32, shape, dim)


def split(x):
    hi = x.astype(BF16)
    return hi, (x - hi.astype(F32)).astype(BF16)


def dot3(a, b, dims=(((1,), (0,)), ((), ()))):
    ca, cb = dims[0][0][0], dims[0][1][0]
    left = jnp.concatenate([a[0], a[1], a[0]], axis=ca)
    right = jnp.concatenate([b[0], b[0], b[1]], axis=cb)
    return lax.dot_general(left, right, dims, preferred_element_type=F32)


def by_parity(x):
    lane = iota((4, LANES), 1)
    first, second = x[0:4], x[4:8]
    even = jnp.where(lane < 64, first, pltpu.roll(second, 64, 1))
    odd = jnp.where(lane < 64, pltpu.roll(first, 64, 1), second)
    return even, odd


def owner_of_row():
    row = iota((LANES, LANES), 0)
    return (2 * row) % LANES + row // 64


def prep_kernel(owner_hbm, offset_hbm, state_hbm, msg_ref, rank_ref, owner_ref, offset_ref, sems):
    rows_of = msg_ref.reshape(NDEV * MSG, LANES)
    state_copy = pltpu.make_async_copy(state_hbm, msg_ref.at[:, 0:STATE_ROWS, :], sems.at[0])
    owner_copy = pltpu.make_async_copy(owner_hbm, owner_ref, sems.at[1])
    offset_copy = pltpu.make_async_copy(offset_hbm, offset_ref, sems.at[2])
    owner_copy.start()
    offset_copy.start()
    state_copy.start()
    owner_copy.wait()
    offset_copy.wait()
    row_owner = owner_of_row()
    before = jnp.where(iota((LANES, LANES), 0) < iota((LANES, LANES), 1), 1.0, 0.0).astype(BF16)
    slot = iota((8, NOBS), 0).astype(F32)
    tables = []
    for b in range(2):
        hot = []
        ranks = []
        count = jnp.zeros((LANES, 1), F32)
        for t in range(NOBS // LANES):
            own = owner_ref[b : b + 1, t * LANES : (t + 1) * LANES]
            is_own = jnp.where(own == row_owner, 1.0, 0.0)
            ahead = jnp.dot(is_own.astype(BF16), before, preferred_element_type=F32) + count
            ranks.append(jnp.sum(is_own * ahead, axis=0, keepdims=True))
            count = count + jnp.sum(is_own, axis=1, keepdims=True)
            hot.append(is_own.astype(BF16))
        hot = jnp.concatenate(hot, axis=1)
        rank = jnp.concatenate(ranks, axis=1)
        rank_ref[b : b + 1, :] = rank
        here = rank == slot
        off = offset_ref[b : b + 1, :]
        parts = [(off // LANES).astype(F32), (off % LANES).astype(F32)]
        rows = jnp.concatenate([jnp.where(here, p, 0.0).astype(BF16) for p in parts], axis=0)
        tables.append(
            lax.dot_general(rows, hot, (((1,), (1,)), ((), ())), preferred_element_type=F32)
        )
    pad = jnp.zeros((LANES - 16, LANES), F32)
    tile_of = jnp.concatenate([tables[0][0:8], tables[1][0:8], pad], axis=0).T.astype(jnp.int32)
    lane_of = jnp.concatenate([tables[0][8:16], tables[1][8:16], pad], axis=0).T.astype(jnp.int32)
    state_copy.wait()
    even_rows = []
    odd_rows = []
    for r in range(2):
        groups = []
        for g in range(16):
            want_tile = tile_of[g * 8 : g * 8 + 8, :]
            want_lane = lane_of[g * 8 : g * 8 + 8, :]
            first = 16 * g if g < 8 else 16 * (g - 8) + 1
            acc = jnp.zeros((8, LANES), F32)
            for c in range(TILES):
                x = rows_of[pl.ds(first * MSG + c * 2 + r, 8, stride=2 * MSG), :]
                acc = jnp.where(want_tile == c, jnp.take_along_axis(x, want_lane, axis=1), acc)
            groups.append(acc)
        found = jnp.concatenate(groups, axis=0).T
        for b in range(2):
            even, odd = by_parity(found[b * 8 : b * 8 + 8])
            even_rows.append(even)
            odd_rows.append(odd)
    even_rows = jnp.concatenate(even_rows, axis=0)
    odd_rows = jnp.concatenate(odd_rows, axis=0)

    def fill(d, _):
        rows_of[pl.ds(d * (2 * MSG) + STATE_ROWS, OBS_ROWS), :] = even_rows
        rows_of[pl.ds(d * (2 * MSG) + MSG + STATE_ROWS, OBS_ROWS), :] = odd_rows
        return 0

    lax.fori_loop(0, NDEV // 2, fill, 0, unroll=8)


def field_kernel(me_ref, owner_ref, offset_ref, value_ref, error_ref, rank_ref, field_ref):
    odd_device = me_ref[0] % 2 == 1
    row_owner = owner_of_row()
    slot = iota((8, NOBS), 0).astype(F32)
    for b in range(2):
        hot = jnp.concatenate(
            [
                jnp.where(owner_ref[b : b + 1, t * LANES : (t + 1) * LANES] == row_owner, 1.0, 0.0).astype(BF16)
                for t in range(NOBS // LANES)
            ],
            axis=1,
        )
        here = rank_ref[b : b + 1, :] == slot
        rows = []
        for x in (offset_ref[b : b + 1, :].astype(F32), value_ref[b : b + 1, :], error_ref[b : b + 1, :]):
            rest = x
            for _ in range(3):
                part = rest.astype(BF16).astype(F32)
                rows.append(jnp.where(here, part, 0.0).astype(BF16))
                rest = rest - part
        t = lax.dot_general(
            jnp.concatenate(rows, axis=0), hot, (((1,), (1,)), ((), ())), preferred_element_type=F32
        )
        for f in range(3):
            at = f * 24
            even, odd = by_parity((t[at : at + 8] + t[at + 8 : at + 16]) + t[at + 16 : at + 24])
            same = jnp.where(odd_device, odd, even)
            other = jnp.where(odd_device, even, odd)
            field_ref[(b * 3 + f) * 8 : (b * 3 + f) * 8 + 8, :] = jnp.concatenate([same, other], axis=0)


def columns(row):
    return jnp.broadcast_to(row, (LANES, LANES)).T


def stats(raw, value, error):
    mean = jnp.sum(raw, axis=0, keepdims=True) * (1.0 / MEMBERS)
    anom = raw - mean
    varian = jnp.sum(anom * anom, axis=0, keepdims=True) * (1.0 / (MEMBERS - 1)) + 1e-06
    total = varian + error
    shrink = jnp.sqrt(error / total)
    scale = -1.0 / ((MEMBERS - 1) * total * (1.0 + shrink))
    push = anom - (value - mean) * (1.0 + shrink)
    return anom, anom * scale, push


def owner_weights(me_ref, table_ref):
    table8 = jnp.broadcast_to(table_ref[...], (8, LANES))
    par = me_ref[0] % 2
    delta = me_ref[0] // 2 - iota((8, LANES), 1) % 64
    steps = jnp.abs(delta)
    far = jnp.take_along_axis(table8, steps, axis=1)[0:1]
    near = jnp.take_along_axis(table8, jnp.maximum(steps - 1, 0), axis=1)[0:1]
    other = jnp.take_along_axis(table8, jnp.abs(2 * delta + 2 * par - 1) // 2, axis=1)[0:1]
    ahead = delta[0:1] > 0
    return jnp.where(ahead, near, far), jnp.where(ahead, far, near), jnp.where(ahead, 0.0, 1.0), other


def field(field_ref, b, f, lo, hi):
    base = (b * 3 + f) * 8
    return jnp.concatenate([field_ref[base + i : base + i + 1, :] for i in range(lo, hi)], axis=1)


def obs_columns(ref, stride, first, b):
    return jnp.concatenate(
        [
            jnp.concatenate(
                [ref[pl.ds(first + r * 8 + b * 4 + s, NDEV, stride=stride), :] for r in range(2)], axis=0
            )
            for s in range(4)
        ],
        axis=1,
    )


def state_columns(recv_ref, at):
    return jnp.concatenate(
        [
            jnp.concatenate(
                [recv_ref[pl.ds((at + h) * 2 + r, NDEV, stride=MSG), :] for r in range(2)], axis=0
            )
            for h in range(WIDE // LANES)
        ],
        axis=1,
    )


def centre(raw):
    return raw - jnp.sum(raw, axis=0, keepdims=True) * (1.0 / MEMBERS)


def same_gain(cov, at, thr, low, high):
    pieces = []
    for k in range(4):
        line = []
        for h in range(WIDE // LANES):
            c = cov[k * LANES : (k + 1) * LANES, h * LANES : (h + 1) * LANES]
            place = (iota((LANES, LANES), 1) + (at + h) * LANES).astype(F32)
            line.append(c * jnp.where(place >= thr[k * LANES : (k + 1) * LANES, :], high, low))
        pieces.append(jnp.concatenate(line, axis=1))
    return split(jnp.concatenate(pieces, axis=0))


def first_kernel(me_ref, table_ref, field_ref, recv_ref, new_ref, left_hi, left_lo, push_hi, push_lo, thr, low, high):
    w_low, w_high, shift, _ = owner_weights(me_ref, table_ref)
    low[...] = columns(w_low)
    high[...] = columns(w_high)
    _, scaled, push = stats(
        obs_columns(recv_ref, MSG, STATE_ROWS, 0), field(field_ref, 0, 1, 0, 4), field(field_ref, 0, 2, 0, 4)
    )
    left_hi[...], left_lo[...] = split(scaled.T)
    push_hi[...], push_lo[...] = split(push)
    off = field(field_ref, 0, 0, 0, 4)
    for s in range(4):
        thr[s * LANES : (s + 1) * LANES, :] = columns(off[:, s * LANES : (s + 1) * LANES] + shift)

    def tile(t, _):
        at = t * (WIDE // LANES)
        raw = state_columns(recv_ref, at)
        cov = dot3((left_hi[...], left_lo[...]), split(centre(raw)))
        gain = same_gain(cov, at, thr, low[...], high[...])
        raw = raw + dot3((push_hi[...], push_lo[...]), gain)
        new_ref[:, pl.ds(pl.multiple_of(t * WIDE, WIDE), WIDE)] = raw
        return 0

    lax.fori_loop(0, NV_DEV // WIDE, tile, 0, unroll=2)


def main_kernel(
    me_ref, table_ref, field_ref, recv_ref, other_ref, new_ref, out_ref,
    left_hi, left_lo, push_hi, push_lo, const_hi, const_lo, thr, low, high, off_col, raw2,
):
    par = me_ref[0] % 2
    table = jnp.broadcast_to(table_ref[...], (LANES, LANES))
    w_low, w_high, shift, w_other = owner_weights(me_ref, table_ref)
    w_other4 = jnp.concatenate([w_other] * 4, axis=1)

    def load_obs(b):
        return jnp.concatenate(
            [obs_columns(recv_ref, MSG, STATE_ROWS, b), obs_columns(other_ref, OBS_ROWS, 0, b)], axis=1
        )

    def block_setup(b, raw):
        _, scaled, push = stats(raw, field(field_ref, b, 1, 0, 8), field(field_ref, b, 2, 0, 8))
        left_hi[...], left_lo[...] = split(scaled.T)
        ph, pw = split(push)
        push_hi[...] = ph
        push_lo[...] = pw
        weighted = split(scaled[:, HALF:] * w_other4)
        const = dot3((ph[:, HALF:], pw[:, HALF:]), weighted, (((1,), (1,)), ((), ())))
        const_hi[b, :, :], const_lo[b, :, :] = split(const)

    low[...] = columns(w_low)
    high[...] = columns(w_high)
    off1 = field(field_ref, 0, 0, 0, 8)
    off2 = field(field_ref, 1, 0, 0, 8)
    for s in range(8):
        off_col[s * LANES : (s + 1) * LANES, :] = columns(off1[:, s * LANES : (s + 1) * LANES])
    for s in range(4):
        thr[s * LANES : (s + 1) * LANES, :] = columns(off2[:, s * LANES : (s + 1) * LANES] + shift)
    block_setup(0, load_obs(0))
    raw2[...] = load_obs(1)

    d = iota((LANES, LANES), 1) % 64 - iota((LANES, LANES), 0) % 64
    ad = jnp.abs(d)
    far = jnp.take_along_axis(table, ad, axis=1)
    near = jnp.take_along_axis(table, jnp.maximum(ad - 1, 0), axis=1)
    sign = jnp.where(d > 0, 1.0, jnp.where(d < 0, -1.0, 0.0))
    to_same = jnp.take_along_axis(table, jnp.abs(2 * d + 2 * par - 1) // 2, axis=1)
    to_other = jnp.take_along_axis(table, jnp.abs(2 * d + 1 - 2 * par) // 2, axis=1)
    for t in range(NOBS // OBS_WIDE):
        raw = raw2[:, t * OBS_WIDE : (t + 1) * OBS_WIDE]
        cov = dot3((left_hi[...], left_lo[...]), split(centre(raw)))
        in_same = t < NOBS // OBS_WIDE // 2
        pieces = []
        for k in range(8):
            line = []
            for h in range(OBS_WIDE // LANES):
                c = cov[k * LANES : (k + 1) * LANES, h * LANES : (h + 1) * LANES]
                if (k < 4) == in_same:
                    at = t * OBS_WIDE + h * LANES
                    gap = off2[:, at : at + LANES] - off_col[k * LANES : (k + 1) * LANES, :]
                    w = jnp.where(gap * sign >= 0.0, far, near)
                else:
                    w = to_same if in_same else to_other
                line.append(c * w)
            pieces.append(jnp.concatenate(line, axis=1))
        gain = split(jnp.concatenate(pieces, axis=0))
        raw2[:, t * OBS_WIDE : (t + 1) * OBS_WIDE] = raw + dot3((push_hi[...], push_lo[...]), gain)
    block_setup(1, raw2[...])

    def tile(t, _):
        at = t * (WIDE // LANES)
        before = split(centre(state_columns(recv_ref, at)))
        raw = new_ref[:, pl.ds(pl.multiple_of(t * WIDE, WIDE), WIDE)]
        raw = raw + dot3((const_hi[0], const_lo[0]), before)
        centred = split(centre(raw))
        cov = dot3((left_hi[0:HALF, :], left_lo[0:HALF, :]), centred)
        gain = same_gain(cov, at, thr, low[...], high[...])
        left = (
            jnp.concatenate([push_hi[:, 0:HALF], const_hi[1]], axis=1),
            jnp.concatenate([push_lo[:, 0:HALF], const_lo[1]], axis=1),
        )
        right = tuple(jnp.concatenate([g, c], axis=0) for g, c in zip(gain, centred))
        raw = raw + dot3(left, right)
        for h in range(WIDE // LANES):
            for r in range(2):
                out_ref[pl.ds((at + h) * 2 + r, NDEV, stride=STATE_ROWS), :] = raw[
                    r * NDEV : (r + 1) * NDEV, h * LANES : (h + 1) * LANES
                ]
        return 0

    lax.fori_loop(0, NV_DEV // WIDE, tile, 0, unroll=2)


VMEM = pl.BlockSpec(memory_space=pltpu.VMEM)
SMEM = pl.BlockSpec(memory_space=pltpu.SMEM)
HBM = pl.BlockSpec(memory_space=pltpu.HBM)


def params(mib):
    return pltpu.CompilerParams(vmem_limit_bytes=mib * 1024 * 1024)


def cost(flops, bytes_accessed):
    return pl.CostEstimate(flops=flops, bytes_accessed=bytes_accessed, transcendentals=0)


def prep(owner, offset, state):
    return pl.pallas_call(
        prep_kernel,
        out_shape=(
            jax.ShapeDtypeStruct((NDEV, MSG, LANES), F32),
            jax.ShapeDtypeStruct((2, NOBS), F32),
        ),
        in_specs=[HBM] * 3,
        out_specs=(VMEM, VMEM),
        scratch_shapes=[
            pltpu.VMEM((2, NOBS), jnp.int32),
            pltpu.VMEM((2, NOBS), jnp.int32),
            pltpu.SemaphoreType.DMA((3,)),
        ],
        compiler_params=params(60),
        name="prep",
    )(owner, offset, state)


def fields_of(me, owner, offset, value, error, rank):
    return pl.pallas_call(
        field_kernel,
        out_shape=jax.ShapeDtypeStruct((48, LANES), F32),
        in_specs=[SMEM] + [VMEM] * 5,
        out_specs=VMEM,
        compiler_params=params(16),
        cost_estimate=cost(2**27, 2**20),
        name="fields",
    )(me, owner, offset, value, error, rank)


def assimilate_first(me, table, fields, recv):
    return pl.pallas_call(
        first_kernel,
        out_shape=jax.ShapeDtypeStruct((MEMBERS, NV_DEV), F32),
        in_specs=[SMEM] + [VMEM] * 3,
        out_specs=VMEM,
        scratch_shapes=[
            pltpu.VMEM((HALF, MEMBERS), BF16),
            pltpu.VMEM((HALF, MEMBERS), BF16),
            pltpu.VMEM((MEMBERS, HALF), BF16),
            pltpu.VMEM((MEMBERS, HALF), BF16),
            pltpu.VMEM((HALF, LANES), F32),
            pltpu.VMEM((LANES, LANES), F32),
            pltpu.VMEM((LANES, LANES), F32),
        ],
        compiler_params=params(VMEM_MIB),
        cost_estimate=cost(3 * 2**31, 5 * 2**20),
        name="first",
    )(me, table, fields, recv)


def assimilate(me, table, fields, recv, other, new):
    return pl.pallas_call(
        main_kernel,
        out_shape=jax.ShapeDtypeStruct((NDEV * STATE_ROWS, LANES), F32),
        in_specs=[SMEM] + [VMEM] * 5,
        out_specs=VMEM,
        scratch_shapes=[
            pltpu.VMEM((NOBS, MEMBERS), BF16),
            pltpu.VMEM((NOBS, MEMBERS), BF16),
            pltpu.VMEM((MEMBERS, NOBS), BF16),
            pltpu.VMEM((MEMBERS, NOBS), BF16),
            pltpu.VMEM((2, MEMBERS, MEMBERS), BF16),
            pltpu.VMEM((2, MEMBERS, MEMBERS), BF16),
            pltpu.VMEM((HALF, LANES), F32),
            pltpu.VMEM((LANES, LANES), F32),
            pltpu.VMEM((LANES, LANES), F32),
            pltpu.VMEM((NOBS, LANES), F32),
            pltpu.VMEM((MEMBERS, NOBS), F32),
        ],
        compiler_params=params(VMEM_MIB),
        cost_estimate=cost(9 * 2**31, 9 * 2**20),
        name="assimilate",
    )(me, table, fields, recv, other, new)


def body(prior_state, obs_value, obs_error, obs_owner, obs_offset, taper_table):
    axes = ("mem", "var")
    me = lax.axis_index(axes).astype(jnp.int32).reshape(1)
    table = jnp.pad(taper_table, (0, LANES - taper_table.shape[0])).reshape(1, LANES)
    state = prior_state.reshape(2, NDEV * TILES, LANES).transpose(1, 0, 2).reshape(NDEV, STATE_ROWS, LANES)
    msg, rank = prep(obs_owner, obs_offset, state)
    recv = lax.all_to_all(msg, axes, split_axis=0, concat_axis=0, tiled=True)
    fields = fields_of(me, obs_owner, obs_offset, obs_value, obs_error, rank)
    mine = recv[:, STATE_ROWS:, :].reshape(NDEV * OBS_ROWS, LANES)
    other = lax.ppermute(mine, axes, [(i, i ^ 1) for i in range(NDEV)])
    recv = recv.reshape(NDEV * MSG, LANES)
    new = assimilate_first(me, table, fields, recv)
    new = assimilate(me, table, fields, recv, other, new)
    back = lax.all_to_all(
        new.reshape(NDEV, STATE_ROWS, LANES), axes, split_axis=0, concat_axis=0, tiled=True
    )
    rows = back.reshape(NDEV * TILES, 2, LANES).transpose(1, 0, 2)
    rows = with_layout_constraint(rows, Layout(major_to_minor=(1, 0, 2)))
    return rows.reshape(2, NDEV * NV_DEV)


def solution(mesh):
    in_specs = (P(("mem", "var"), None), P(), P(), P(), P(), P())
    out_specs = P(("mem", "var"), None)
    return jax.shard_map(body, mesh=mesh, in_specs=in_specs, out_specs=out_specs, check_vma=False)
```

```python
import functools

import jax
import jax.numpy as jnp
from jax import lax
from jax.experimental import pallas as pl
from jax.experimental.layout import Layout, with_layout_constraint
from jax.experimental.pallas import tpu as pltpu
from jax.sharding import PartitionSpec as P

MEMBERS = 256
NDEV = 128
NOBS = 1024
HALF = NOBS // 2
NV_DEV = 2048
LANES = 128
TILES = NV_DEV // LANES
STATE_ROWS = 2 * TILES
OBS_ROWS = 16
MSG = STATE_ROWS + OBS_ROWS
PIECES = 4
WIDE = 1024
OBS_WIDE = 512
F32 = jnp.float32
BF16 = jnp.bfloat16
VMEM_MIB = 32


def iota(shape, dim):
    return lax.broadcasted_iota(jnp.int32, shape, dim)


def split(x):
    hi = x.astype(BF16)
    return hi, (x - hi.astype(F32)).astype(BF16)


def dot3(a, b, dims=(((1,), (0,)), ((), ()))):
    ca, cb = dims[0][0][0], dims[0][1][0]
    left = jnp.concatenate([a[0], a[1], a[0]], axis=ca)
    right = jnp.concatenate([b[0], b[0], b[1]], axis=cb)
    return lax.dot_general(left, right, dims, preferred_element_type=F32)


def by_parity(x):
    lane = iota((4, LANES), 1)
    first, second = x[0:4], x[4:8]
    even = jnp.where(lane < 64, first, pltpu.roll(second, 64, 1))
    odd = jnp.where(lane < 64, pltpu.roll(first, 64, 1), second)
    return even, odd


def owner_of_row():
    row = iota((LANES, LANES), 0)
    return (2 * row) % LANES + row // 64


def prep_kernel(
    me_ref, owner_hbm, offset_hbm, state_hbm, msg_ref, rank_ref, owner_ref, offset_ref, small_sems, state_sems
):
    rows_of = msg_ref.reshape(NDEV * MSG, LANES)
    owner_copy = pltpu.make_async_copy(owner_hbm, owner_ref, small_sems.at[0])
    offset_copy = pltpu.make_async_copy(offset_hbm, offset_ref, small_sems.at[1])
    owner_copy.start()
    offset_copy.start()
    share = NDEV // PIECES
    pieces = [
        pltpu.make_async_copy(
            state_hbm.at[p * share : (p + 1) * share],
            msg_ref.at[p * share : (p + 1) * share, 0:STATE_ROWS, :],
            state_sems.at[p],
        )
        for p in range(PIECES)
    ]
    for piece in pieces:
        piece.start()
    owner_copy.wait()
    offset_copy.wait()
    row_owner = iota((LANES, LANES), 0)
    before = jnp.where(iota((LANES, LANES), 0) < iota((LANES, LANES), 1), 1.0, 0.0).astype(BF16)
    slot = iota((8, NOBS), 0).astype(F32)
    tables = []
    for b in range(2):
        hot = []
        ranks = []
        count = jnp.zeros((LANES, 1), F32)
        for t in range(NOBS // LANES):
            own = owner_ref[b : b + 1, t * LANES : (t + 1) * LANES]
            is_own = jnp.where(own == row_owner, 1.0, 0.0)
            ahead = jnp.dot(is_own.astype(BF16), before, preferred_element_type=F32) + count
            ranks.append(jnp.sum(is_own * ahead, axis=0, keepdims=True))
            count = count + jnp.sum(is_own, axis=1, keepdims=True)
            hot.append(is_own.astype(BF16))
        hot = jnp.concatenate(hot, axis=1)
        rank = jnp.concatenate(ranks, axis=1)
        rank_ref[b : b + 1, :] = rank
        here = rank == slot
        off = offset_ref[b : b + 1, :]
        parts = [(off // LANES).astype(F32), (off % LANES).astype(F32)]
        rows = jnp.concatenate([jnp.where(here, p, 0.0).astype(BF16) for p in parts], axis=0)
        tables.append(
            lax.dot_general(rows, hot, (((1,), (1,)), ((), ())), preferred_element_type=F32)
        )
    pad = jnp.zeros((LANES - 16, LANES), F32)
    tile_of = jnp.concatenate([tables[0][0:8], tables[1][0:8], pad], axis=0).T.astype(jnp.int32)
    lane_of = jnp.concatenate([tables[0][8:16], tables[1][8:16], pad], axis=0).T.astype(jnp.int32)
    groups = [[], []]
    for g in range(NDEV // 8):
        if g % (share // 8) == 0:
            pieces[g // (share // 8)].wait()
        want_tile = tile_of[g * 8 : g * 8 + 8, :]
        want_lane = lane_of[g * 8 : g * 8 + 8, :]
        for r in range(2):
            acc = jnp.zeros((8, LANES), F32)
            for c in range(TILES):
                x = rows_of[pl.ds(g * 8 * MSG + c * 2 + r, 8, stride=MSG), :]
                acc = jnp.where(want_tile == c, jnp.take_along_axis(x, want_lane, axis=1), acc)
            groups[r].append(acc)
    lane = iota((8, LANES), 1)
    parity_order = (2 * lane) % LANES + lane // 64
    even_rows = []
    odd_rows = []
    for r in range(2):
        found = jnp.concatenate(groups[r], axis=0).T
        for b in range(2):
            even, odd = by_parity(jnp.take_along_axis(found[b * 8 : b * 8 + 8], parity_order, axis=1))
            even_rows.append(even)
            odd_rows.append(odd)
    even_rows = jnp.concatenate(even_rows, axis=0)
    odd_rows = jnp.concatenate(odd_rows, axis=0)
    for d in range(NDEV):
        msg_ref[d, STATE_ROWS:MSG, :] = odd_rows if d % 2 else even_rows


def field_kernel(me_ref, owner_ref, offset_ref, value_ref, error_ref, rank_ref, recv_ref, mine_ref, field_ref):
    for d in range(NDEV):
        mine_ref[d, :, :] = recv_ref[d, STATE_ROWS:MSG, :]
    odd_device = me_ref[0] % 2 == 1
    row_owner = owner_of_row()
    slot = iota((8, NOBS), 0).astype(F32)
    for b in range(2):
        hot = jnp.concatenate(
            [
                jnp.where(owner_ref[b : b + 1, t * LANES : (t + 1) * LANES] == row_owner, 1.0, 0.0).astype(BF16)
                for t in range(NOBS // LANES)
            ],
            axis=1,
        )
        here = rank_ref[b : b + 1, :] == slot
        rows = []
        for x in (offset_ref[b : b + 1, :].astype(F32), value_ref[b : b + 1, :], error_ref[b : b + 1, :]):
            rest = x
            for _ in range(3):
                part = rest.astype(BF16).astype(F32)
                rows.append(jnp.where(here, part, 0.0).astype(BF16))
                rest = rest - part
        t = lax.dot_general(
            jnp.concatenate(rows, axis=0), hot, (((1,), (1,)), ((), ())), preferred_element_type=F32
        )
        for f in range(3):
            at = f * 24
            even, odd = by_parity((t[at : at + 8] + t[at + 8 : at + 16]) + t[at + 16 : at + 24])
            same = jnp.where(odd_device, odd, even)
            other = jnp.where(odd_device, even, odd)
            field_ref[(b * 3 + f) * 8 : (b * 3 + f) * 8 + 8, :] = jnp.concatenate([same, other], axis=0)


def columns(row):
    return jnp.broadcast_to(row, (LANES, LANES)).T


def stats(raw, value, error):
    mean = jnp.sum(raw, axis=0, keepdims=True) * (1.0 / MEMBERS)
    anom = raw - mean
    varian = jnp.sum(anom * anom, axis=0, keepdims=True) * (1.0 / (MEMBERS - 1)) + 1e-06
    total = varian + error
    shrink = jnp.sqrt(error / total)
    scale = -1.0 / ((MEMBERS - 1) * total * (1.0 + shrink))
    push = anom - (value - mean) * (1.0 + shrink)
    return anom, anom * scale, push


def owner_weights(me_ref, table_ref):
    table8 = jnp.broadcast_to(table_ref[...], (8, LANES))
    par = me_ref[0] % 2
    delta = me_ref[0] // 2 - iota((8, LANES), 1) % 64
    steps = jnp.abs(delta)
    far = jnp.take_along_axis(table8, steps, axis=1)[0:1]
    near = jnp.take_along_axis(table8, jnp.maximum(steps - 1, 0), axis=1)[0:1]
    other = jnp.take_along_axis(table8, jnp.abs(2 * delta + 2 * par - 1) // 2, axis=1)[0:1]
    ahead = delta[0:1] > 0
    return jnp.where(ahead, near, far), jnp.where(ahead, far, near), jnp.where(ahead, 0.0, 1.0), other


def field(field_ref, b, f, lo, hi):
    base = (b * 3 + f) * 8
    return jnp.concatenate([field_ref[base + i : base + i + 1, :] for i in range(lo, hi)], axis=1)


def obs_columns(ref, stride, first, b):
    return jnp.concatenate(
        [
            jnp.concatenate(
                [ref[pl.ds(first + r * 8 + b * 4 + s, NDEV, stride=stride), :] for r in range(2)], axis=0
            )
            for s in range(4)
        ],
        axis=1,
    )


def state_columns(recv_ref, at):
    return jnp.concatenate(
        [
            jnp.concatenate(
                [recv_ref[pl.ds((at + h) * 2 + r, NDEV, stride=MSG), :] for r in range(2)], axis=0
            )
            for h in range(WIDE // LANES)
        ],
        axis=1,
    )


def same_gain(cov, at, thr, low, high):
    pieces = []
    for k in range(4):
        line = []
        for h in range(WIDE // LANES):
            c = cov[k * LANES : (k + 1) * LANES, h * LANES : (h + 1) * LANES]
            place = (iota((LANES, LANES), 1) + (at + h) * LANES).astype(F32)
            line.append(c * jnp.where(place >= thr[k * LANES : (k + 1) * LANES, :], high, low))
        pieces.append(jnp.concatenate(line, axis=1))
    return split(jnp.concatenate(pieces, axis=0))


def first_kernel(me_ref, table_ref, field_ref, recv_ref, new_ref, left_hi, left_lo, push_hi, push_lo, thr, low, high):
    w_low, w_high, shift, _ = owner_weights(me_ref, table_ref)
    low[...] = columns(w_low)
    high[...] = columns(w_high)
    _, scaled, push = stats(
        obs_columns(recv_ref, MSG, STATE_ROWS, 0), field(field_ref, 0, 1, 0, 4), field(field_ref, 0, 2, 0, 4)
    )
    left_hi[...], left_lo[...] = split(scaled.T)
    push_hi[...], push_lo[...] = split(push)
    off = field(field_ref, 0, 0, 0, 4)
    for s in range(4):
        thr[s * LANES : (s + 1) * LANES, :] = columns(off[:, s * LANES : (s + 1) * LANES] + shift)

    def tile(t, _):
        at = t * (WIDE // LANES)
        raw = state_columns(recv_ref, at)
        cov = dot3((left_hi[...], left_lo[...]), split(raw))
        gain = same_gain(cov, at, thr, low[...], high[...])
        raw = raw + dot3((push_hi[...], push_lo[...]), gain)
        new_ref[:, pl.ds(pl.multiple_of(t * WIDE, WIDE), WIDE)] = raw
        return 0

    lax.fori_loop(0, NV_DEV // WIDE, tile, 0, unroll=2)


def main_kernel(
    me_ref, table_ref, field_ref, recv_ref, other_ref, new_ref, out_ref,
    left_hi, left_lo, push_hi, push_lo, const_hi, const_lo, thr, low, high, off_col, raw2,
):
    par = me_ref[0] % 2
    table = jnp.broadcast_to(table_ref[...], (LANES, LANES))
    w_low, w_high, shift, w_other = owner_weights(me_ref, table_ref)
    w_other4 = jnp.concatenate([w_other] * 4, axis=1)

    def load_obs(b):
        return jnp.concatenate(
            [obs_columns(recv_ref, MSG, STATE_ROWS, b), obs_columns(other_ref, OBS_ROWS, 0, b)], axis=1
        )

    def block_setup(b, raw):
        _, scaled, push = stats(raw, field(field_ref, b, 1, 0, 8), field(field_ref, b, 2, 0, 8))
        left_hi[...], left_lo[...] = split(scaled.T)
        ph, pw = split(push)
        push_hi[...] = ph
        push_lo[...] = pw
        weighted = split(scaled[:, HALF:] * w_other4)
        const = dot3((ph[:, HALF:], pw[:, HALF:]), weighted, (((1,), (1,)), ((), ())))
        const_hi[b, :, :], const_lo[b, :, :] = split(const)

    low[...] = columns(w_low)
    high[...] = columns(w_high)
    off1 = field(field_ref, 0, 0, 0, 8)
    off2 = field(field_ref, 1, 0, 0, 8)
    for s in range(8):
        off_col[s * LANES : (s + 1) * LANES, :] = columns(off1[:, s * LANES : (s + 1) * LANES])
    for s in range(4):
        thr[s * LANES : (s + 1) * LANES, :] = columns(off2[:, s * LANES : (s + 1) * LANES] + shift)
    block_setup(0, load_obs(0))
    raw2[...] = load_obs(1)

    d = iota((LANES, LANES), 1) % 64 - iota((LANES, LANES), 0) % 64
    ad = jnp.abs(d)
    far = jnp.take_along_axis(table, ad, axis=1)
    near = jnp.take_along_axis(table, jnp.maximum(ad - 1, 0), axis=1)
    sign = jnp.where(d > 0, 1.0, jnp.where(d < 0, -1.0, 0.0))
    to_same = jnp.take_along_axis(table, jnp.abs(2 * d + 2 * par - 1) // 2, axis=1)
    to_other = jnp.take_along_axis(table, jnp.abs(2 * d + 1 - 2 * par) // 2, axis=1)
    for t in range(NOBS // OBS_WIDE):
        raw = raw2[:, t * OBS_WIDE : (t + 1) * OBS_WIDE]
        cov = dot3((left_hi[...], left_lo[...]), split(raw))
        in_same = t < NOBS // OBS_WIDE // 2
        pieces = []
        for k in range(8):
            line = []
            for h in range(OBS_WIDE // LANES):
                c = cov[k * LANES : (k + 1) * LANES, h * LANES : (h + 1) * LANES]
                if (k < 4) == in_same:
                    at = t * OBS_WIDE + h * LANES
                    gap = off2[:, at : at + LANES] - off_col[k * LANES : (k + 1) * LANES, :]
                    w = jnp.where(gap * sign >= 0.0, far, near)
                else:
                    w = to_same if in_same else to_other
                line.append(c * w)
            pieces.append(jnp.concatenate(line, axis=1))
        gain = split(jnp.concatenate(pieces, axis=0))
        raw2[:, t * OBS_WIDE : (t + 1) * OBS_WIDE] = raw + dot3((push_hi[...], push_lo[...]), gain)
    block_setup(1, raw2[...])

    def tile(t, _):
        at = t * (WIDE // LANES)
        before = split(state_columns(recv_ref, at))
        raw = new_ref[:, pl.ds(pl.multiple_of(t * WIDE, WIDE), WIDE)]
        raw = raw + dot3((const_hi[0], const_lo[0]), before)
        centred = split(raw)
        cov = dot3((left_hi[0:HALF, :], left_lo[0:HALF, :]), centred)
        gain = same_gain(cov, at, thr, low[...], high[...])
        left = (
            jnp.concatenate([push_hi[:, 0:HALF], const_hi[1]], axis=1),
            jnp.concatenate([push_lo[:, 0:HALF], const_lo[1]], axis=1),
        )
        right = tuple(jnp.concatenate([g, c], axis=0) for g, c in zip(gain, centred))
        raw = raw + dot3(left, right)
        for h in range(WIDE // LANES):
            for r in range(2):
                out_ref[pl.ds((at + h) * 2 + r, NDEV, stride=STATE_ROWS), :] = raw[
                    r * NDEV : (r + 1) * NDEV, h * LANES : (h + 1) * LANES
                ]
        return 0

    lax.fori_loop(0, NV_DEV // WIDE, tile, 0, unroll=2)


VMEM = pl.BlockSpec(memory_space=pltpu.VMEM)
SMEM = pl.BlockSpec(memory_space=pltpu.SMEM)
HBM = pl.BlockSpec(memory_space=pltpu.HBM)


def params(mib):
    return pltpu.CompilerParams(vmem_limit_bytes=mib * 1024 * 1024)


def cost(flops, bytes_accessed):
    return pl.CostEstimate(flops=flops, bytes_accessed=bytes_accessed, transcendentals=0)


def in_hbm(x):
    return pltpu.with_memory_space_constraint(x, pltpu.HBM)


def prep(me, owner, offset, state):
    return pl.pallas_call(
        prep_kernel,
        out_shape=(
            jax.ShapeDtypeStruct((NDEV, MSG, LANES), F32),
            jax.ShapeDtypeStruct((2, NOBS), F32),
        ),
        in_specs=[SMEM] + [HBM] * 3,
        out_specs=(VMEM, VMEM),
        scratch_shapes=[
            pltpu.VMEM((2, NOBS), jnp.int32),
            pltpu.VMEM((2, NOBS), jnp.int32),
            pltpu.SemaphoreType.DMA((2,)),
            pltpu.SemaphoreType.DMA((PIECES,)),
        ],
        compiler_params=params(16),
        name="prep",
    )(me, owner, offset, state)


def sort_out(me, owner, offset, value, error, rank, recv):
    return pl.pallas_call(
        field_kernel,
        out_shape=(
            jax.ShapeDtypeStruct((NDEV, OBS_ROWS, LANES), F32),
            jax.ShapeDtypeStruct((48, LANES), F32),
        ),
        in_specs=[SMEM] + [VMEM] * 6,
        out_specs=(VMEM, VMEM),
        compiler_params=params(16),
        name="fields",
    )(me, owner, offset, value, error, rank, recv)


def assimilate_first(me, table, fields, recv):
    return pl.pallas_call(
        first_kernel,
        out_shape=jax.ShapeDtypeStruct((MEMBERS, NV_DEV), F32),
        in_specs=[SMEM] + [VMEM] * 3,
        out_specs=VMEM,
        scratch_shapes=[
            pltpu.VMEM((HALF, MEMBERS), BF16),
            pltpu.VMEM((HALF, MEMBERS), BF16),
            pltpu.VMEM((MEMBERS, HALF), BF16),
            pltpu.VMEM((MEMBERS, HALF), BF16),
            pltpu.VMEM((HALF, LANES), F32),
            pltpu.VMEM((LANES, LANES), F32),
            pltpu.VMEM((LANES, LANES), F32),
        ],
        compiler_params=params(VMEM_MIB),
        cost_estimate=cost(3 * 2**31, 5 * 2**20),
        name="first",
    )(me, table, fields, recv)


def assimilate(me, table, fields, recv, other, new):
    return pl.pallas_call(
        main_kernel,
        out_shape=jax.ShapeDtypeStruct((NDEV * STATE_ROWS, LANES), F32),
        in_specs=[SMEM] + [VMEM] * 5,
        out_specs=VMEM,
        scratch_shapes=[
            pltpu.VMEM((NOBS, MEMBERS), BF16),
            pltpu.VMEM((NOBS, MEMBERS), BF16),
            pltpu.VMEM((MEMBERS, NOBS), BF16),
            pltpu.VMEM((MEMBERS, NOBS), BF16),
            pltpu.VMEM((2, MEMBERS, MEMBERS), BF16),
            pltpu.VMEM((2, MEMBERS, MEMBERS), BF16),
            pltpu.VMEM((HALF, LANES), F32),
            pltpu.VMEM((LANES, LANES), F32),
            pltpu.VMEM((LANES, LANES), F32),
            pltpu.VMEM((NOBS, LANES), F32),
            pltpu.VMEM((MEMBERS, NOBS), F32),
        ],
        compiler_params=params(VMEM_MIB),
        cost_estimate=cost(9 * 2**31, 9 * 2**20),
        name="assimilate",
    )(me, table, fields, recv, other, new)


def body(prior_state, obs_value, obs_error, obs_owner, obs_offset, taper_table):
    axes = ("mem", "var")
    me = lax.axis_index(axes).astype(jnp.int32).reshape(1)
    state = prior_state.reshape(2, NDEV * TILES, LANES).transpose(1, 0, 2).reshape(NDEV, STATE_ROWS, LANES)
    msg, rank = prep(me, in_hbm(obs_owner), in_hbm(obs_offset), in_hbm(state))
    recv = lax.all_to_all(msg, axes, split_axis=0, concat_axis=0, tiled=True)
    table = jnp.pad(taper_table, (0, LANES - taper_table.shape[0])).reshape(1, LANES)
    mine, fields = sort_out(me, obs_owner, obs_offset, obs_value, obs_error, rank, recv)
    other = lax.ppermute(mine, axes, [(i, i ^ 1) for i in range(NDEV)]).reshape(NDEV * OBS_ROWS, LANES)
    recv = recv.reshape(NDEV * MSG, LANES)
    new = assimilate_first(me, table, fields, recv)
    new = assimilate(me, table, fields, recv, other, new)
    back = lax.all_to_all(
        new.reshape(NDEV, STATE_ROWS, LANES), axes, split_axis=0, concat_axis=0, tiled=True
    )
    rows = back.reshape(NDEV * TILES, 2, LANES).transpose(1, 0, 2)
    rows = with_layout_constraint(rows, Layout(major_to_minor=(1, 0, 2)))
    return rows.reshape(2, NDEV * NV_DEV)


def solution(mesh):
    in_specs = (P(("mem", "var"), None), P(), P(), P(), P(), P())
    out_specs = P(("mem", "var"), None)
    return jax.shard_map(body, mesh=mesh, in_specs=in_specs, out_specs=out_specs, check_vma=False)
```

```python
import functools

import jax
import jax.numpy as jnp
from jax import lax
from jax.experimental import pallas as pl
from jax.experimental.layout import Layout, with_layout_constraint
from jax.experimental.pallas import tpu as pltpu
from jax.sharding import PartitionSpec as P

MEMBERS = 256
NDEV = 128
NOBS = 1024
HALF = NOBS // 2
NV_DEV = 2048
LANES = 128
TILES = NV_DEV // LANES
STATE_ROWS = 2 * TILES
OBS_ROWS = 16
MSG = STATE_ROWS + OBS_ROWS
PIECES = 1
WIDE = 1024
F32 = jnp.float32
BF16 = jnp.bfloat16
VMEM_MIB = 32


def iota(shape, dim):
    return lax.broadcasted_iota(jnp.int32, shape, dim)


def split(x):
    hi = x.astype(BF16)
    return hi, (x - hi.astype(F32)).astype(BF16)


BOTH_LANES = (((1,), (1,)), ((), ()))


def dot3(a, b, dims=(((1,), (0,)), ((), ()))):
    ca, cb = dims[0][0][0], dims[0][1][0]
    left = jnp.concatenate([a[0], a[1], a[0]], axis=ca)
    right = jnp.concatenate([b[0], b[0], b[1]], axis=cb)
    return lax.dot_general(left, right, dims, preferred_element_type=F32)


def by_parity(x):
    lane = iota((4, LANES), 1)
    first, second = x[0:4], x[4:8]
    even = jnp.where(lane < 64, first, pltpu.roll(second, 64, 1))
    odd = jnp.where(lane < 64, pltpu.roll(first, 64, 1), second)
    return even, odd


def owner_of_row():
    row = iota((LANES, LANES), 0)
    return (2 * row) % LANES + row // 64


def prep_kernel(
    me_ref, owner_hbm, offset_hbm, state_hbm, msg_ref, rank_ref, owner_ref, offset_ref, small_sems, state_sems
):
    rows_of = msg_ref.reshape(NDEV * MSG, LANES)
    owner_copy = pltpu.make_async_copy(owner_hbm, owner_ref, small_sems.at[0])
    offset_copy = pltpu.make_async_copy(offset_hbm, offset_ref, small_sems.at[1])
    owner_copy.start()
    offset_copy.start()
    share = NDEV // PIECES
    pieces = [
        pltpu.make_async_copy(
            state_hbm.at[p * share : (p + 1) * share],
            msg_ref.at[p * share : (p + 1) * share, 0:STATE_ROWS, :],
            state_sems.at[p],
        )
        for p in range(PIECES)
    ]
    for piece in pieces:
        piece.start()
    owner_copy.wait()
    offset_copy.wait()
    row_owner = iota((LANES, LANES), 0)
    before = jnp.where(iota((LANES, LANES), 0) < iota((LANES, LANES), 1), 1.0, 0.0).astype(BF16)
    slot = iota((8, NOBS), 0).astype(F32)
    tables = []
    for b in range(2):
        hot = []
        ranks = []
        count = jnp.zeros((LANES, 1), F32)
        for t in range(NOBS // LANES):
            own = owner_ref[b : b + 1, t * LANES : (t + 1) * LANES]
            is_own = jnp.where(own == row_owner, 1.0, 0.0)
            ahead = jnp.dot(is_own.astype(BF16), before, preferred_element_type=F32) + count
            ranks.append(jnp.sum(is_own * ahead, axis=0, keepdims=True))
            count = count + jnp.sum(is_own, axis=1, keepdims=True)
            hot.append(is_own.astype(BF16))
        hot = jnp.concatenate(hot, axis=1)
        rank = jnp.concatenate(ranks, axis=1)
        rank_ref[b : b + 1, :] = rank
        here = rank == slot
        off = offset_ref[b : b + 1, :]
        parts = [(off // LANES).astype(F32), (off % LANES).astype(F32)]
        rows = jnp.concatenate([jnp.where(here, p, 0.0).astype(BF16) for p in parts], axis=0)
        tables.append(
            lax.dot_general(rows, hot, (((1,), (1,)), ((), ())), preferred_element_type=F32)
        )
    pad = jnp.zeros((LANES - 16, LANES), F32)
    tile_of = jnp.concatenate([tables[0][0:8], tables[1][0:8], pad], axis=0).T.astype(jnp.int32)
    lane_of = jnp.concatenate([tables[0][8:16], tables[1][8:16], pad], axis=0).T.astype(jnp.int32)
    groups = [[], []]
    for g in range(NDEV // 8):
        if g % (share // 8) == 0:
            pieces[g // (share // 8)].wait()
        want_tile = tile_of[g * 8 : g * 8 + 8, :]
        want_lane = lane_of[g * 8 : g * 8 + 8, :]
        for r in range(2):
            acc = jnp.zeros((8, LANES), F32)
            for c in range(TILES):
                x = rows_of[pl.ds(g * 8 * MSG + c * 2 + r, 8, stride=MSG), :]
                acc = jnp.where(want_tile == c, jnp.take_along_axis(x, want_lane, axis=1), acc)
            groups[r].append(acc)
    lane = iota((8, LANES), 1)
    parity_order = (2 * lane) % LANES + lane // 64
    even_rows = []
    odd_rows = []
    for r in range(2):
        found = jnp.concatenate(groups[r], axis=0).T
        for b in range(2):
            even, odd = by_parity(jnp.take_along_axis(found[b * 8 : b * 8 + 8], parity_order, axis=1))
            even_rows.append(even)
            odd_rows.append(odd)
    even_rows = jnp.concatenate(even_rows, axis=0)
    odd_rows = jnp.concatenate(odd_rows, axis=0)
    for d in range(NDEV):
        msg_ref[d, STATE_ROWS:MSG, :] = odd_rows if d % 2 else even_rows


def field_kernel(me_ref, owner_ref, offset_ref, value_ref, error_ref, rank_ref, recv_ref, mine_ref, field_ref):
    for d in range(NDEV):
        mine_ref[d, :, :] = recv_ref[d, STATE_ROWS:MSG, :]
    odd_device = me_ref[0] % 2 == 1
    row_owner = owner_of_row()
    slot = iota((8, NOBS), 0).astype(F32)
    for b in range(2):
        hot = jnp.concatenate(
            [
                jnp.where(owner_ref[b : b + 1, t * LANES : (t + 1) * LANES] == row_owner, 1.0, 0.0).astype(BF16)
                for t in range(NOBS // LANES)
            ],
            axis=1,
        )
        here = rank_ref[b : b + 1, :] == slot
        rows = []
        for x in (offset_ref[b : b + 1, :].astype(F32), value_ref[b : b + 1, :], error_ref[b : b + 1, :]):
            rest = x
            for _ in range(3):
                part = rest.astype(BF16).astype(F32)
                rows.append(jnp.where(here, part, 0.0).astype(BF16))
                rest = rest - part
        t = lax.dot_general(
            jnp.concatenate(rows, axis=0), hot, (((1,), (1,)), ((), ())), preferred_element_type=F32
        )
        for f in range(3):
            at = f * 24
            even, odd = by_parity((t[at : at + 8] + t[at + 8 : at + 16]) + t[at + 16 : at + 24])
            same = jnp.where(odd_device, odd, even)
            other = jnp.where(odd_device, even, odd)
            field_ref[(b * 3 + f) * 8 : (b * 3 + f) * 8 + 8, :] = jnp.concatenate([same, other], axis=0)


def columns(row):
    return jnp.broadcast_to(row, (LANES, LANES)).T


def stats(raw, value, error):
    mean = jnp.sum(raw, axis=0, keepdims=True) * (1.0 / MEMBERS)
    anom = raw - mean
    varian = jnp.sum(anom * anom, axis=0, keepdims=True) * (1.0 / (MEMBERS - 1)) + 1e-06
    total = varian + error
    shrink = jnp.sqrt(error / total)
    scale = -1.0 / ((MEMBERS - 1) * total * (1.0 + shrink))
    push = anom - (value - mean) * (1.0 + shrink)
    return anom, anom * scale, push


def owner_weights(me_ref, table_ref):
    table8 = jnp.broadcast_to(table_ref[...], (8, LANES))
    par = me_ref[0] % 2
    delta = me_ref[0] // 2 - iota((8, LANES), 1) % 64
    steps = jnp.abs(delta)
    far = jnp.take_along_axis(table8, steps, axis=1)[0:1]
    near = jnp.take_along_axis(table8, jnp.maximum(steps - 1, 0), axis=1)[0:1]
    other = jnp.take_along_axis(table8, jnp.abs(2 * delta + 2 * par - 1) // 2, axis=1)[0:1]
    ahead = delta[0:1] > 0
    return jnp.where(ahead, near, far), jnp.where(ahead, far, near), jnp.where(ahead, 0.0, 1.0), other


def field(field_ref, b, f, lo, hi):
    base = (b * 3 + f) * 8
    return jnp.concatenate([field_ref[base + i : base + i + 1, :] for i in range(lo, hi)], axis=1)


def obs_columns(ref, stride, first, b):
    return jnp.concatenate(
        [
            jnp.concatenate(
                [ref[pl.ds(first + r * 8 + b * 4 + s, NDEV, stride=stride), :] for r in range(2)], axis=0
            )
            for s in range(4)
        ],
        axis=1,
    )


def state_columns(recv_ref, at):
    return jnp.concatenate(
        [
            jnp.concatenate(
                [recv_ref[pl.ds((at + h) * 2 + r, NDEV, stride=MSG), :] for r in range(2)], axis=0
            )
            for h in range(WIDE // LANES)
        ],
        axis=1,
    )


def same_gain(cov, at, thr, low, high):
    pieces = []
    for k in range(4):
        line = []
        for h in range(WIDE // LANES):
            c = cov[k * LANES : (k + 1) * LANES, h * LANES : (h + 1) * LANES]
            place = (iota((LANES, LANES), 1) + (at + h) * LANES).astype(F32)
            line.append(c * jnp.where(place >= thr[k * LANES : (k + 1) * LANES, :], high, low))
        pieces.append(jnp.concatenate(line, axis=1))
    return split(jnp.concatenate(pieces, axis=0))


def first_kernel(
    me_ref, table_ref, field_ref, recv_ref, new_ref, left_hi, left_lo, push_hi, push_lo, low, high, thr
):
    w_low, w_high, shift, _ = owner_weights(me_ref, table_ref)
    low[...] = columns(w_low)
    high[...] = columns(w_high)
    _, scaled, push = stats(
        obs_columns(recv_ref, MSG, STATE_ROWS, 0), field(field_ref, 0, 1, 0, 4), field(field_ref, 0, 2, 0, 4)
    )
    left_hi[...], left_lo[...] = split(scaled.T)
    push_hi[...], push_lo[...] = split(push)
    off = field(field_ref, 0, 0, 0, 4)
    for s in range(4):
        thr[s * LANES : (s + 1) * LANES, :] = columns(off[:, s * LANES : (s + 1) * LANES] + shift)

    for t in range(NV_DEV // WIDE):
        at = t * (WIDE // LANES)
        raw = state_columns(recv_ref, at)
        cov = dot3((left_hi[...], left_lo[...]), split(raw))
        gain = same_gain(cov, at, thr, low[...], high[...])
        raw = raw + dot3((push_hi[...], push_lo[...]), gain)
        new_ref[:, t * WIDE : (t + 1) * WIDE] = raw


def main_kernel(
    me_ref, table_ref, field_ref, recv_ref, other_ref, new_ref,
    first_left_hi, first_left_lo, first_push_hi, first_push_lo, low, high, out_ref,
    left_hi, left_lo, push_hi, push_lo, left2_hi, left2_lo, push2_hi, push2_lo, const_hi, const_lo, thr,
):
    par = me_ref[0] % 2
    table = jnp.broadcast_to(table_ref[...], (LANES, LANES))
    _, _, shift, w_other = owner_weights(me_ref, table_ref)
    w_other4 = jnp.concatenate([w_other] * 4, axis=1)

    def set_const(b, scaled, push):
        const = dot3(push, split(scaled * w_other4), BOTH_LANES)
        const_hi[b, :, :], const_lo[b, :, :] = split(const)

    off1 = field(field_ref, 0, 0, 0, 8)
    off2 = field(field_ref, 1, 0, 0, 8)
    d = iota((LANES, LANES), 1) % 64 - iota((LANES, LANES), 0) % 64
    ad = jnp.abs(d)
    far = jnp.take_along_axis(table, ad, axis=1)
    near = jnp.take_along_axis(table, jnp.maximum(ad - 1, 0), axis=1)
    sign = jnp.where(d > 0, 1.0, jnp.where(d < 0, -1.0, 0.0))
    to_same = jnp.take_along_axis(table, jnp.abs(2 * d + 2 * par - 1) // 2, axis=1)
    to_other = jnp.take_along_axis(table, jnp.abs(2 * d + 1 - 2 * par) // 2, axis=1)

    def alike(cov, first):
        pieces = []
        for k in range(4):
            at = first + k * LANES
            column = columns(off1[:, at : at + LANES])
            line = []
            for h in range(4):
                gap = off2[:, first + h * LANES : first + (h + 1) * LANES] - column
                c = cov[k * LANES : (k + 1) * LANES, h * LANES : (h + 1) * LANES]
                line.append(c * jnp.where(gap * sign >= 0.0, far, near))
            pieces.append(jnp.concatenate(line, axis=1))
        return jnp.concatenate(pieces, axis=0)

    def unlike(cov, weight):
        return cov * jnp.concatenate([jnp.concatenate([weight] * 4, axis=1)] * 4, axis=0)

    same2 = obs_columns(recv_ref, MSG, STATE_ROWS, 1)
    other2 = obs_columns(other_ref, OBS_ROWS, 0, 1)
    same2_parts = split(same2)
    other2_parts = split(other2)
    left_same = (first_left_hi[...], first_left_lo[...])
    cov_same = dot3(left_same, same2_parts)
    _, scaled, push = stats(
        obs_columns(other_ref, OBS_ROWS, 0, 0), field(field_ref, 0, 1, 4, 8), field(field_ref, 0, 2, 4, 8)
    )
    left_hi[...], left_lo[...] = split(scaled.T)
    push_hi[...], push_lo[...] = split(push)
    left_other = (left_hi[...], left_lo[...])
    cov_other = dot3(left_other, same2_parts)
    push_all = (
        jnp.concatenate([first_push_hi[...], push_hi[...]], axis=1),
        jnp.concatenate([first_push_lo[...], push_lo[...]], axis=1),
    )
    gain = split(jnp.concatenate([alike(cov_same, 0), unlike(cov_other, to_same)], axis=0))
    same2 = same2 + dot3(push_all, gain)
    cov_same = dot3(left_same, other2_parts)
    cov_other = dot3(left_other, other2_parts)
    set_const(0, scaled, (push_hi[...], push_lo[...]))
    _, scaled, push = stats(same2, field(field_ref, 1, 1, 0, 4), field(field_ref, 1, 2, 0, 4))
    left2_hi[...], left2_lo[...] = split(scaled.T)
    push2_hi[...], push2_lo[...] = split(push)
    for s in range(4):
        thr[s * LANES : (s + 1) * LANES, :] = columns(off2[:, s * LANES : (s + 1) * LANES] + shift)
    gain = split(jnp.concatenate([unlike(cov_same, to_other), alike(cov_other, HALF)], axis=0))
    other2 = other2 + dot3(push_all, gain)
    _, scaled, push = stats(other2, field(field_ref, 1, 1, 4, 8), field(field_ref, 1, 2, 4, 8))
    set_const(1, scaled, split(push))

    for t in range(NV_DEV // WIDE):
        at = t * (WIDE // LANES)
        before = split(state_columns(recv_ref, at))
        raw = new_ref[:, t * WIDE : (t + 1) * WIDE]
        raw = raw + dot3((const_hi[0], const_lo[0]), before)
        centred = split(raw)
        cov = dot3((left2_hi[...], left2_lo[...]), centred)
        gain = same_gain(cov, at, thr, low[...], high[...])
        left = (
            jnp.concatenate([push2_hi[...], const_hi[1]], axis=1),
            jnp.concatenate([push2_lo[...], const_lo[1]], axis=1),
        )
        right = tuple(jnp.concatenate([g, c], axis=0) for g, c in zip(gain, centred))
        raw = raw + dot3(left, right)
        for h in range(WIDE // LANES):
            for r in range(2):
                out_ref[pl.ds((at + h) * 2 + r, NDEV, stride=STATE_ROWS), :] = raw[
                    r * NDEV : (r + 1) * NDEV, h * LANES : (h + 1) * LANES
                ]


VMEM = pl.BlockSpec(memory_space=pltpu.VMEM)
SMEM = pl.BlockSpec(memory_space=pltpu.SMEM)
HBM = pl.BlockSpec(memory_space=pltpu.HBM)


def params(mib):
    return pltpu.CompilerParams(vmem_limit_bytes=mib * 1024 * 1024)


def cost(flops, bytes_accessed):
    return pl.CostEstimate(flops=flops, bytes_accessed=bytes_accessed, transcendentals=0)


def in_hbm(x):
    return pltpu.with_memory_space_constraint(x, pltpu.HBM)


def prep(me, owner, offset, state):
    return pl.pallas_call(
        prep_kernel,
        out_shape=(
            jax.ShapeDtypeStruct((NDEV, MSG, LANES), F32),
            jax.ShapeDtypeStruct((2, NOBS), F32),
        ),
        in_specs=[SMEM] + [HBM] * 3,
        out_specs=(VMEM, VMEM),
        scratch_shapes=[
            pltpu.VMEM((2, NOBS), jnp.int32),
            pltpu.VMEM((2, NOBS), jnp.int32),
            pltpu.SemaphoreType.DMA((2,)),
            pltpu.SemaphoreType.DMA((PIECES,)),
        ],
        compiler_params=params(16),
        name="prep",
    )(me, owner, offset, state)


def sort_out(me, owner, offset, value, error, rank, recv):
    return pl.pallas_call(
        field_kernel,
        out_shape=(
            jax.ShapeDtypeStruct((NDEV, OBS_ROWS, LANES), F32),
            jax.ShapeDtypeStruct((48, LANES), F32),
        ),
        in_specs=[SMEM] + [VMEM] * 6,
        out_specs=(VMEM, VMEM),
        compiler_params=params(16),
        name="fields",
    )(me, owner, offset, value, error, rank, recv)


def assimilate_first(me, table, fields, recv):
    return pl.pallas_call(
        first_kernel,
        out_shape=(
            jax.ShapeDtypeStruct((MEMBERS, NV_DEV), F32),
            jax.ShapeDtypeStruct((HALF, MEMBERS), BF16),
            jax.ShapeDtypeStruct((HALF, MEMBERS), BF16),
            jax.ShapeDtypeStruct((MEMBERS, HALF), BF16),
            jax.ShapeDtypeStruct((MEMBERS, HALF), BF16),
            jax.ShapeDtypeStruct((LANES, LANES), F32),
            jax.ShapeDtypeStruct((LANES, LANES), F32),
        ),
        in_specs=[SMEM] + [VMEM] * 3,
        out_specs=(VMEM,) * 7,
        scratch_shapes=[pltpu.VMEM((HALF, LANES), F32)],
        compiler_params=params(VMEM_MIB),
        cost_estimate=cost(3 * 2**31, 5 * 2**20),
        name="first",
    )(me, table, fields, recv)


def assimilate(me, table, fields, recv, other, first):
    return pl.pallas_call(
        main_kernel,
        out_shape=jax.ShapeDtypeStruct((NDEV * STATE_ROWS, LANES), F32),
        in_specs=[SMEM] + [VMEM] * 11,
        out_specs=VMEM,
        scratch_shapes=[
            pltpu.VMEM((HALF, MEMBERS), BF16),
            pltpu.VMEM((HALF, MEMBERS), BF16),
            pltpu.VMEM((MEMBERS, HALF), BF16),
            pltpu.VMEM((MEMBERS, HALF), BF16),
            pltpu.VMEM((HALF, MEMBERS), BF16),
            pltpu.VMEM((HALF, MEMBERS), BF16),
            pltpu.VMEM((MEMBERS, HALF), BF16),
            pltpu.VMEM((MEMBERS, HALF), BF16),
            pltpu.VMEM((2, MEMBERS, MEMBERS), BF16),
            pltpu.VMEM((2, MEMBERS, MEMBERS), BF16),
            pltpu.VMEM((HALF, LANES), F32),
        ],
        compiler_params=params(VMEM_MIB),
        cost_estimate=cost(9 * 2**31, 9 * 2**20),
        name="assimilate",
    )(me, table, fields, recv, other, *first)


def body(prior_state, obs_value, obs_error, obs_owner, obs_offset, taper_table):
    axes = ("mem", "var")
    me = lax.axis_index(axes).astype(jnp.int32).reshape(1)
    state = prior_state.reshape(2, NDEV * TILES, LANES).transpose(1, 0, 2).reshape(NDEV, STATE_ROWS, LANES)
    msg, rank = prep(me, in_hbm(obs_owner), in_hbm(obs_offset), in_hbm(state))
    recv = lax.all_to_all(msg, axes, split_axis=0, concat_axis=0, tiled=True)
    table = jnp.pad(taper_table, (0, LANES - taper_table.shape[0])).reshape(1, LANES)
    mine, fields = sort_out(me, obs_owner, obs_offset, obs_value, obs_error, rank, recv)
    other = lax.ppermute(mine, axes, [(i, i ^ 1) for i in range(NDEV)]).reshape(NDEV * OBS_ROWS, LANES)
    recv = recv.reshape(NDEV * MSG, LANES)
    first = assimilate_first(me, table, fields, recv)
    new = assimilate(me, table, fields, recv, other, first)
    back = lax.all_to_all(
        new.reshape(NDEV, STATE_ROWS, LANES), axes, split_axis=0, concat_axis=0, tiled=True
    )
    rows = back.reshape(NDEV * TILES, 2, LANES).transpose(1, 0, 2)
    rows = with_layout_constraint(rows, Layout(major_to_minor=(1, 0, 2)))
    return rows.reshape(2, NDEV * NV_DEV)


def solution(mesh):
    in_specs = (P(("mem", "var"), None), P(), P(), P(), P(), P())
    out_specs = P(("mem", "var"), None)
    return jax.shard_map(body, mesh=mesh, in_specs=in_specs, out_specs=out_specs, check_vma=False)
```

```python
import functools

import jax
import jax.numpy as jnp
from jax import lax
from jax.experimental import pallas as pl
from jax.experimental.layout import Layout, with_layout_constraint
from jax.experimental.pallas import tpu as pltpu
from jax.sharding import PartitionSpec as P

MEMBERS = 256
NDEV = 128
NOBS = 1024
HALF = NOBS // 2
NV_DEV = 2048
LANES = 128
TILES = NV_DEV // LANES
STATE_ROWS = 2 * TILES
OBS_ROWS = 16
MSG = STATE_ROWS + OBS_ROWS
PIECES = 1
WIDE = 1024
F32 = jnp.float32
BF16 = jnp.bfloat16
VMEM_MIB = 32


def iota(shape, dim):
    return lax.broadcasted_iota(jnp.int32, shape, dim)


def split(x):
    hi = x.astype(BF16)
    return hi, (x - hi.astype(F32)).astype(BF16)


BOTH_LANES = (((1,), (1,)), ((), ()))


def dot3(a, b, dims=(((1,), (0,)), ((), ()))):
    ca, cb = dims[0][0][0], dims[0][1][0]
    left = jnp.concatenate([a[0], a[1], a[0]], axis=ca)
    right = jnp.concatenate([b[0], b[0], b[1]], axis=cb)
    return lax.dot_general(left, right, dims, preferred_element_type=F32)


def by_parity(x):
    lane = iota((4, LANES), 1)
    first, second = x[0:4], x[4:8]
    even = jnp.where(lane < 64, first, pltpu.roll(second, 64, 1))
    odd = jnp.where(lane < 64, pltpu.roll(first, 64, 1), second)
    return even, odd


def owner_of_row():
    row = iota((LANES, LANES), 0)
    return (2 * row) % LANES + row // 64


def prep_kernel(
    me_ref, owner_hbm, offset_hbm, state_hbm, msg_ref, rank_ref, owner_ref, offset_ref, small_sems, state_sems
):
    rows_of = msg_ref.reshape(NDEV * MSG, LANES)
    owner_copy = pltpu.make_async_copy(owner_hbm, owner_ref, small_sems.at[0])
    offset_copy = pltpu.make_async_copy(offset_hbm, offset_ref, small_sems.at[1])
    owner_copy.start()
    offset_copy.start()
    share = NDEV // PIECES
    pieces = [
        pltpu.make_async_copy(
            state_hbm.at[p * share : (p + 1) * share],
            msg_ref.at[p * share : (p + 1) * share, 0:STATE_ROWS, :],
            state_sems.at[p],
        )
        for p in range(PIECES)
    ]
    for piece in pieces:
        piece.start()
    owner_copy.wait()
    offset_copy.wait()
    row_owner = iota((LANES, LANES), 0)
    before = jnp.where(iota((LANES, LANES), 0) < iota((LANES, LANES), 1), 1.0, 0.0).astype(BF16)
    slot = iota((8, NOBS), 0).astype(F32)
    tables = []
    for b in range(2):
        hot = []
        ranks = []
        count = jnp.zeros((LANES, 1), F32)
        for t in range(NOBS // LANES):
            own = owner_ref[b : b + 1, t * LANES : (t + 1) * LANES]
            is_own = jnp.where(own == row_owner, 1.0, 0.0)
            ahead = jnp.dot(is_own.astype(BF16), before, preferred_element_type=F32) + count
            ranks.append(jnp.sum(is_own * ahead, axis=0, keepdims=True))
            count = count + jnp.sum(is_own, axis=1, keepdims=True)
            hot.append(is_own.astype(BF16))
        hot = jnp.concatenate(hot, axis=1)
        rank = jnp.concatenate(ranks, axis=1)
        rank_ref[b : b + 1, :] = rank
        here = rank == slot
        off = offset_ref[b : b + 1, :]
        gap = [jnp.zeros((8, NOBS), F32)]
        tile_rows = jnp.where(here, (off // LANES).astype(F32), 0.0)
        lane_rows = jnp.where(here, (off % LANES).astype(F32), 0.0)
        rows = gap * b + [tile_rows] + gap * 7 + [lane_rows] + gap * (7 - b)
        tables.append(
            lax.dot_general(
                hot, jnp.concatenate(rows, axis=0).astype(BF16), BOTH_LANES, preferred_element_type=F32
            )
        )
    place = tables[0] + tables[1]
    tile_of = place.astype(jnp.int32)
    lane_of = pltpu.roll(place, 64, 1).astype(jnp.int32)
    groups = [[], []]
    for g in range(NDEV // 8):
        if g % (share // 8) == 0:
            pieces[g // (share // 8)].wait()
        want_tile = tile_of[g * 8 : g * 8 + 8, :]
        want_lane = lane_of[g * 8 : g * 8 + 8, :]
        for r in range(2):
            acc = jnp.zeros((8, LANES), F32)
            for c in range(TILES):
                x = rows_of[pl.ds(g * 8 * MSG + c * 2 + r, 8, stride=MSG), :]
                acc = jnp.where(want_tile == c, jnp.take_along_axis(x, want_lane, axis=1), acc)
            groups[r].append(acc)
    lane = iota((8, LANES), 1)
    parity_order = (2 * lane) % LANES + lane // 64
    even_rows = []
    odd_rows = []
    for r in range(2):
        found = jnp.concatenate(groups[r], axis=0).T
        for b in range(2):
            even, odd = by_parity(jnp.take_along_axis(found[b * 8 : b * 8 + 8], parity_order, axis=1))
            even_rows.append(even)
            odd_rows.append(odd)
    even_rows = jnp.concatenate(even_rows, axis=0)
    odd_rows = jnp.concatenate(odd_rows, axis=0)
    for d in range(NDEV):
        msg_ref[d, STATE_ROWS:MSG, :] = odd_rows if d % 2 else even_rows


def field_kernel(me_ref, owner_ref, offset_ref, value_ref, error_ref, rank_ref, recv_ref, mine_ref, field_ref):
    for d in range(NDEV):
        mine_ref[d, :, :] = recv_ref[d, STATE_ROWS:MSG, :]
    odd_device = me_ref[0] % 2 == 1
    row_owner = owner_of_row()
    slot = iota((8, NOBS), 0).astype(F32)
    for b in range(2):
        hot = jnp.concatenate(
            [
                jnp.where(owner_ref[b : b + 1, t * LANES : (t + 1) * LANES] == row_owner, 1.0, 0.0).astype(BF16)
                for t in range(NOBS // LANES)
            ],
            axis=1,
        )
        here = rank_ref[b : b + 1, :] == slot
        rows = []
        for x in (offset_ref[b : b + 1, :].astype(F32), value_ref[b : b + 1, :], error_ref[b : b + 1, :]):
            rest = x
            for _ in range(3):
                part = rest.astype(BF16).astype(F32)
                rows.append(jnp.where(here, part, 0.0).astype(BF16))
                rest = rest - part
        t = lax.dot_general(
            jnp.concatenate(rows, axis=0), hot, (((1,), (1,)), ((), ())), preferred_element_type=F32
        )
        for f in range(3):
            at = f * 24
            even, odd = by_parity((t[at : at + 8] + t[at + 8 : at + 16]) + t[at + 16 : at + 24])
            same = jnp.where(odd_device, odd, even)
            other = jnp.where(odd_device, even, odd)
            field_ref[(b * 3 + f) * 8 : (b * 3 + f) * 8 + 8, :] = jnp.concatenate([same, other], axis=0)


def columns(row):
    return jnp.broadcast_to(row, (LANES, LANES)).T


def stats(raw, value, error):
    mean = jnp.sum(raw, axis=0, keepdims=True) * (1.0 / MEMBERS)
    anom = raw - mean
    varian = jnp.sum(anom * anom, axis=0, keepdims=True) * (1.0 / (MEMBERS - 1)) + 1e-06
    total = varian + error
    shrink = jnp.sqrt(error / total)
    scale = -1.0 / ((MEMBERS - 1) * total * (1.0 + shrink))
    push = anom - (value - mean) * (1.0 + shrink)
    return anom, anom * scale, push


def owner_weights(me_ref, table_ref):
    table8 = jnp.broadcast_to(table_ref[...], (8, LANES))
    par = me_ref[0] % 2
    delta = me_ref[0] // 2 - iota((8, LANES), 1) % 64
    steps = jnp.abs(delta)
    far = jnp.take_along_axis(table8, steps, axis=1)[0:1]
    near = jnp.take_along_axis(table8, jnp.maximum(steps - 1, 0), axis=1)[0:1]
    other = jnp.take_along_axis(table8, jnp.abs(2 * delta + 2 * par - 1) // 2, axis=1)[0:1]
    ahead = delta[0:1] > 0
    return jnp.where(ahead, near, far), jnp.where(ahead, far, near), jnp.where(ahead, 0.0, 1.0), other


def field(field_ref, b, f, lo, hi):
    base = (b * 3 + f) * 8
    return jnp.concatenate([field_ref[base + i : base + i + 1, :] for i in range(lo, hi)], axis=1)


def obs_columns(ref, stride, first, b):
    return jnp.concatenate(
        [
            jnp.concatenate(
                [ref[pl.ds(first + r * 8 + b * 4 + s, NDEV, stride=stride), :] for r in range(2)], axis=0
            )
            for s in range(4)
        ],
        axis=1,
    )


def state_columns(recv_ref, at):
    return jnp.concatenate(
        [
            jnp.concatenate(
                [recv_ref[pl.ds((at + h) * 2 + r, NDEV, stride=MSG), :] for r in range(2)], axis=0
            )
            for h in range(WIDE // LANES)
        ],
        axis=1,
    )


def same_gain(cov, at, thr, low, high):
    pieces = []
    for k in range(4):
        line = []
        for h in range(WIDE // LANES):
            c = cov[k * LANES : (k + 1) * LANES, h * LANES : (h + 1) * LANES]
            place = (iota((LANES, LANES), 1) + (at + h) * LANES).astype(F32)
            line.append(c * jnp.where(place >= thr[k * LANES : (k + 1) * LANES, :], high, low))
        pieces.append(jnp.concatenate(line, axis=1))
    return split(jnp.concatenate(pieces, axis=0))


def first_kernel(
    me_ref, table_ref, field_ref, recv_ref, new_ref, left_hi, left_lo, push_hi, push_lo, low, high, thr
):
    w_low, w_high, shift, _ = owner_weights(me_ref, table_ref)
    low[...] = columns(w_low)
    high[...] = columns(w_high)
    _, scaled, push = stats(
        obs_columns(recv_ref, MSG, STATE_ROWS, 0), field(field_ref, 0, 1, 0, 4), field(field_ref, 0, 2, 0, 4)
    )
    left_hi[...], left_lo[...] = split(scaled.T)
    push_hi[...], push_lo[...] = split(push)
    off = field(field_ref, 0, 0, 0, 4)
    for s in range(4):
        thr[s * LANES : (s + 1) * LANES, :] = columns(off[:, s * LANES : (s + 1) * LANES] + shift)

    for t in range(NV_DEV // WIDE):
        at = t * (WIDE // LANES)
        raw = state_columns(recv_ref, at)
        cov = dot3((left_hi[...], left_lo[...]), split(raw))
        gain = same_gain(cov, at, thr, low[...], high[...])
        raw = raw + dot3((push_hi[...], push_lo[...]), gain)
        new_ref[:, t * WIDE : (t + 1) * WIDE] = raw


def main_kernel(
    me_ref, table_ref, field_ref, recv_ref, other_ref, new_ref,
    first_left_hi, first_left_lo, first_push_hi, first_push_lo, low, high, out_ref,
    left_hi, left_lo, push_hi, push_lo, left2_hi, left2_lo, push2_hi, push2_lo, const_hi, const_lo, thr,
):
    par = me_ref[0] % 2
    table = jnp.broadcast_to(table_ref[...], (LANES, LANES))
    _, _, shift, w_other = owner_weights(me_ref, table_ref)
    w_other4 = jnp.concatenate([w_other] * 4, axis=1)

    def set_const(b, scaled, push):
        const = dot3(push, split(scaled * w_other4), BOTH_LANES)
        const_hi[b, :, :], const_lo[b, :, :] = split(const)

    off1 = field(field_ref, 0, 0, 0, 8)
    off2 = field(field_ref, 1, 0, 0, 8)
    d = iota((LANES, LANES), 1) % 64 - iota((LANES, LANES), 0) % 64
    ad = jnp.abs(d)
    far = jnp.take_along_axis(table, ad, axis=1)
    near = jnp.take_along_axis(table, jnp.maximum(ad - 1, 0), axis=1)
    sign = jnp.where(d > 0, 1.0, jnp.where(d < 0, -1.0, 0.0))
    to_same = jnp.take_along_axis(table, jnp.abs(2 * d + 2 * par - 1) // 2, axis=1)
    to_other = jnp.take_along_axis(table, jnp.abs(2 * d + 1 - 2 * par) // 2, axis=1)

    def alike(cov, first):
        pieces = []
        for k in range(4):
            at = first + k * LANES
            column = columns(off1[:, at : at + LANES])
            line = []
            for h in range(4):
                gap = off2[:, first + h * LANES : first + (h + 1) * LANES] - column
                c = cov[k * LANES : (k + 1) * LANES, h * LANES : (h + 1) * LANES]
                line.append(c * jnp.where(gap * sign >= 0.0, far, near))
            pieces.append(jnp.concatenate(line, axis=1))
        return jnp.concatenate(pieces, axis=0)

    def unlike(cov, weight):
        return cov * jnp.concatenate([jnp.concatenate([weight] * 4, axis=1)] * 4, axis=0)

    same2 = obs_columns(recv_ref, MSG, STATE_ROWS, 1)
    other2 = obs_columns(other_ref, OBS_ROWS, 0, 1)
    same2_parts = split(same2)
    other2_parts = split(other2)
    left_same = (first_left_hi[...], first_left_lo[...])
    cov_same = dot3(left_same, same2_parts)
    _, scaled, push = stats(
        obs_columns(other_ref, OBS_ROWS, 0, 0), field(field_ref, 0, 1, 4, 8), field(field_ref, 0, 2, 4, 8)
    )
    left_hi[...], left_lo[...] = split(scaled.T)
    push_hi[...], push_lo[...] = split(push)
    left_other = (left_hi[...], left_lo[...])
    cov_other = dot3(left_other, same2_parts)
    push_all = (
        jnp.concatenate([first_push_hi[...], push_hi[...]], axis=1),
        jnp.concatenate([first_push_lo[...], push_lo[...]], axis=1),
    )
    gain = split(jnp.concatenate([alike(cov_same, 0), unlike(cov_other, to_same)], axis=0))
    same2 = same2 + dot3(push_all, gain)
    cov_same = dot3(left_same, other2_parts)
    cov_other = dot3(left_other, other2_parts)
    set_const(0, scaled, (push_hi[...], push_lo[...]))
    _, scaled, push = stats(same2, field(field_ref, 1, 1, 0, 4), field(field_ref, 1, 2, 0, 4))
    left2_hi[...], left2_lo[...] = split(scaled.T)
    push2_hi[...], push2_lo[...] = split(push)
    for s in range(4):
        thr[s * LANES : (s + 1) * LANES, :] = columns(off2[:, s * LANES : (s + 1) * LANES] + shift)
    gain = split(jnp.concatenate([unlike(cov_same, to_other), alike(cov_other, HALF)], axis=0))
    other2 = other2 + dot3(push_all, gain)
    _, scaled, push = stats(other2, field(field_ref, 1, 1, 4, 8), field(field_ref, 1, 2, 4, 8))
    set_const(1, scaled, split(push))

    for t in range(NV_DEV // WIDE):
        at = t * (WIDE // LANES)
        before = split(state_columns(recv_ref, at))
        raw = new_ref[:, t * WIDE : (t + 1) * WIDE]
        raw = raw + dot3((const_hi[0], const_lo[0]), before)
        centred = split(raw)
        cov = dot3((left2_hi[...], left2_lo[...]), centred)
        gain = same_gain(cov, at, thr, low[...], high[...])
        left = (
            jnp.concatenate([push2_hi[...], const_hi[1]], axis=1),
            jnp.concatenate([push2_lo[...], const_lo[1]], axis=1),
        )
        right = tuple(jnp.concatenate([g, c], axis=0) for g, c in zip(gain, centred))
        raw = raw + dot3(left, right)
        for h in range(WIDE // LANES):
            for r in range(2):
                out_ref[pl.ds((at + h) * 2 + r, NDEV, stride=STATE_ROWS), :] = raw[
                    r * NDEV : (r + 1) * NDEV, h * LANES : (h + 1) * LANES
                ]


VMEM = pl.BlockSpec(memory_space=pltpu.VMEM)
SMEM = pl.BlockSpec(memory_space=pltpu.SMEM)
HBM = pl.BlockSpec(memory_space=pltpu.HBM)


def params(mib):
    return pltpu.CompilerParams(vmem_limit_bytes=mib * 1024 * 1024)


def cost(flops, bytes_accessed):
    return pl.CostEstimate(flops=flops, bytes_accessed=bytes_accessed, transcendentals=0)


def in_hbm(x):
    return pltpu.with_memory_space_constraint(x, pltpu.HBM)


def prep(me, owner, offset, state):
    return pl.pallas_call(
        prep_kernel,
        out_shape=(
            jax.ShapeDtypeStruct((NDEV, MSG, LANES), F32),
            jax.ShapeDtypeStruct((2, NOBS), F32),
        ),
        in_specs=[SMEM] + [HBM] * 3,
        out_specs=(VMEM, VMEM),
        scratch_shapes=[
            pltpu.VMEM((2, NOBS), jnp.int32),
            pltpu.VMEM((2, NOBS), jnp.int32),
            pltpu.SemaphoreType.DMA((2,)),
            pltpu.SemaphoreType.DMA((PIECES,)),
        ],
        compiler_params=params(16),
        name="prep",
    )(me, owner, offset, state)


def sort_out(me, owner, offset, value, error, rank, recv):
    return pl.pallas_call(
        field_kernel,
        out_shape=(
            jax.ShapeDtypeStruct((NDEV, OBS_ROWS, LANES), F32),
            jax.ShapeDtypeStruct((48, LANES), F32),
        ),
        in_specs=[SMEM] + [VMEM] * 6,
        out_specs=(VMEM, VMEM),
        compiler_params=params(16),
        name="fields",
    )(me, owner, offset, value, error, rank, recv)


def assimilate_first(me, table, fields, recv):
    return pl.pallas_call(
        first_kernel,
        out_shape=(
            jax.ShapeDtypeStruct((MEMBERS, NV_DEV), F32),
            jax.ShapeDtypeStruct((HALF, MEMBERS), BF16),
            jax.ShapeDtypeStruct((HALF, MEMBERS), BF16),
            jax.ShapeDtypeStruct((MEMBERS, HALF), BF16),
            jax.ShapeDtypeStruct((MEMBERS, HALF), BF16),
            jax.ShapeDtypeStruct((LANES, LANES), F32),
            jax.ShapeDtypeStruct((LANES, LANES), F32),
        ),
        in_specs=[SMEM] + [VMEM] * 3,
        out_specs=(VMEM,) * 7,
        scratch_shapes=[pltpu.VMEM((HALF, LANES), F32)],
        compiler_params=params(VMEM_MIB),
        cost_estimate=cost(3 * 2**31, 5 * 2**20),
        name="first",
    )(me, table, fields, recv)


def assimilate(me, table, fields, recv, other, first):
    return pl.pallas_call(
        main_kernel,
        out_shape=jax.ShapeDtypeStruct((NDEV * STATE_ROWS, LANES), F32),
        in_specs=[SMEM] + [VMEM] * 11,
        out_specs=VMEM,
        scratch_shapes=[
            pltpu.VMEM((HALF, MEMBERS), BF16),
            pltpu.VMEM((HALF, MEMBERS), BF16),
            pltpu.VMEM((MEMBERS, HALF), BF16),
            pltpu.VMEM((MEMBERS, HALF), BF16),
            pltpu.VMEM((HALF, MEMBERS), BF16),
            pltpu.VMEM((HALF, MEMBERS), BF16),
            pltpu.VMEM((MEMBERS, HALF), BF16),
            pltpu.VMEM((MEMBERS, HALF), BF16),
            pltpu.VMEM((2, MEMBERS, MEMBERS), BF16),
            pltpu.VMEM((2, MEMBERS, MEMBERS), BF16),
            pltpu.VMEM((HALF, LANES), F32),
        ],
        compiler_params=params(VMEM_MIB),
        cost_estimate=cost(9 * 2**31, 9 * 2**20),
        name="assimilate",
    )(me, table, fields, recv, other, *first)


def body(prior_state, obs_value, obs_error, obs_owner, obs_offset, taper_table):
    axes = ("mem", "var")
    me = lax.axis_index(axes).astype(jnp.int32).reshape(1)
    state = prior_state.reshape(2, NDEV * TILES, LANES).transpose(1, 0, 2).reshape(NDEV, STATE_ROWS, LANES)
    msg, rank = prep(me, in_hbm(obs_owner), in_hbm(obs_offset), in_hbm(state))
    recv = lax.all_to_all(msg, axes, split_axis=0, concat_axis=0, tiled=True)
    table = jnp.pad(taper_table, (0, LANES - taper_table.shape[0])).reshape(1, LANES)
    mine, fields = sort_out(me, obs_owner, obs_offset, obs_value, obs_error, rank, recv)
    other = lax.ppermute(mine, axes, [(i, i ^ 1) for i in range(NDEV)]).reshape(NDEV * OBS_ROWS, LANES)
    recv = recv.reshape(NDEV * MSG, LANES)
    first = assimilate_first(me, table, fields, recv)
    new = assimilate(me, table, fields, recv, other, first)
    back = lax.all_to_all(
        new.reshape(NDEV, STATE_ROWS, LANES), axes, split_axis=0, concat_axis=0, tiled=True
    )
    rows = back.reshape(NDEV * TILES, 2, LANES).transpose(1, 0, 2)
    rows = with_layout_constraint(rows, Layout(major_to_minor=(1, 0, 2)))
    return rows.reshape(2, NDEV * NV_DEV)


def solution(mesh):
    in_specs = (P(("mem", "var"), None), P(), P(), P(), P(), P())
    out_specs = P(("mem", "var"), None)
    return jax.shard_map(body, mesh=mesh, in_specs=in_specs, out_specs=out_specs, check_vma=False)
```

```python
import functools

import jax
import jax.numpy as jnp
from jax import lax
from jax.experimental import pallas as pl
from jax.experimental.layout import Layout, with_layout_constraint
from jax.experimental.pallas import tpu as pltpu
from jax.sharding import PartitionSpec as P

MEMBERS = 256
NDEV = 128
NOBS = 1024
HALF = NOBS // 2
NV_DEV = 2048
LANES = 128
TILES = NV_DEV // LANES
STATE_ROWS = 2 * TILES
OBS_ROWS = 16
MSG = STATE_ROWS + OBS_ROWS
PIECES = 1
WIDE = 2048
F32 = jnp.float32
BF16 = jnp.bfloat16
VMEM_MIB = 32


def iota(shape, dim):
    return lax.broadcasted_iota(jnp.int32, shape, dim)


def split(x):
    hi = x.astype(BF16)
    return hi, (x - hi.astype(F32)).astype(BF16)


BOTH_LANES = (((1,), (1,)), ((), ()))


def dot3(a, b, dims=(((1,), (0,)), ((), ()))):
    ca, cb = dims[0][0][0], dims[0][1][0]
    left = jnp.concatenate([a[0], a[1], a[0]], axis=ca)
    right = jnp.concatenate([b[0], b[0], b[1]], axis=cb)
    return lax.dot_general(left, right, dims, preferred_element_type=F32)


def by_parity(x):
    lane = iota((4, LANES), 1)
    first, second = x[0:4], x[4:8]
    even = jnp.where(lane < 64, first, pltpu.roll(second, 64, 1))
    odd = jnp.where(lane < 64, pltpu.roll(first, 64, 1), second)
    return even, odd


def owner_of_row():
    row = iota((LANES, LANES), 0)
    return (2 * row) % LANES + row // 64


def prep_kernel(
    me_ref, owner_hbm, offset_hbm, state_hbm, msg_ref, rank_ref, owner_ref, offset_ref, small_sems, state_sems
):
    rows_of = msg_ref.reshape(NDEV * MSG, LANES)
    owner_copy = pltpu.make_async_copy(owner_hbm, owner_ref, small_sems.at[0])
    offset_copy = pltpu.make_async_copy(offset_hbm, offset_ref, small_sems.at[1])
    owner_copy.start()
    offset_copy.start()
    share = NDEV // PIECES
    pieces = [
        pltpu.make_async_copy(
            state_hbm.at[p * share : (p + 1) * share],
            msg_ref.at[p * share : (p + 1) * share, 0:STATE_ROWS, :],
            state_sems.at[p],
        )
        for p in range(PIECES)
    ]
    for piece in pieces:
        piece.start()
    owner_copy.wait()
    offset_copy.wait()
    row_owner = iota((LANES, LANES), 0)
    before = jnp.where(iota((LANES, LANES), 0) < iota((LANES, LANES), 1), 1.0, 0.0).astype(BF16)
    slot = iota((8, NOBS), 0).astype(F32)
    tables = []
    for b in range(2):
        hot = []
        ranks = []
        count = jnp.zeros((LANES, 1), F32)
        for t in range(NOBS // LANES):
            own = owner_ref[b : b + 1, t * LANES : (t + 1) * LANES]
            is_own = jnp.where(own == row_owner, 1.0, 0.0)
            ahead = jnp.dot(is_own.astype(BF16), before, preferred_element_type=F32) + count
            ranks.append(jnp.sum(is_own * ahead, axis=0, keepdims=True))
            count = count + jnp.sum(is_own, axis=1, keepdims=True)
            hot.append(is_own.astype(BF16))
        hot = jnp.concatenate(hot, axis=1)
        rank = jnp.concatenate(ranks, axis=1)
        rank_ref[b : b + 1, :] = rank
        here = rank == slot
        off = offset_ref[b : b + 1, :]
        gap = [jnp.zeros((8, NOBS), F32)]
        tile_rows = jnp.where(here, (off // LANES).astype(F32), 0.0)
        lane_rows = jnp.where(here, (off % LANES).astype(F32), 0.0)
        rows = gap * b + [tile_rows] + gap * 7 + [lane_rows] + gap * (7 - b)
        tables.append(
            lax.dot_general(
                hot, jnp.concatenate(rows, axis=0).astype(BF16), BOTH_LANES, preferred_element_type=F32
            )
        )
    place = tables[0] + tables[1]
    tile_of = place.astype(jnp.int32)
    lane_of = pltpu.roll(place, 64, 1).astype(jnp.int32)
    groups = [[], []]
    for g in range(NDEV // 8):
        if g % (share // 8) == 0:
            pieces[g // (share // 8)].wait()
        want_tile = tile_of[g * 8 : g * 8 + 8, :]
        want_lane = lane_of[g * 8 : g * 8 + 8, :]
        for r in range(2):
            acc = jnp.zeros((8, LANES), F32)
            for c in range(TILES):
                x = rows_of[pl.ds(g * 8 * MSG + c * 2 + r, 8, stride=MSG), :]
                acc = jnp.where(want_tile == c, jnp.take_along_axis(x, want_lane, axis=1), acc)
            groups[r].append(acc)
    lane = iota((8, LANES), 1)
    parity_order = (2 * lane) % LANES + lane // 64
    even_rows = []
    odd_rows = []
    for r in range(2):
        found = jnp.concatenate(groups[r], axis=0).T
        for b in range(2):
            even, odd = by_parity(jnp.take_along_axis(found[b * 8 : b * 8 + 8], parity_order, axis=1))
            even_rows.append(even)
            odd_rows.append(odd)
    even_rows = jnp.concatenate(even_rows, axis=0)
    odd_rows = jnp.concatenate(odd_rows, axis=0)
    for d in range(NDEV):
        msg_ref[d, STATE_ROWS:MSG, :] = odd_rows if d % 2 else even_rows


def field_kernel(me_ref, owner_ref, offset_ref, value_ref, error_ref, rank_ref, recv_ref, mine_ref, field_ref):
    for d in range(NDEV):
        mine_ref[d, :, :] = recv_ref[d, STATE_ROWS:MSG, :]
    odd_device = me_ref[0] % 2 == 1
    row_owner = owner_of_row()
    slot = iota((8, NOBS), 0).astype(F32)
    for b in range(2):
        hot = jnp.concatenate(
            [
                jnp.where(owner_ref[b : b + 1, t * LANES : (t + 1) * LANES] == row_owner, 1.0, 0.0).astype(BF16)
                for t in range(NOBS // LANES)
            ],
            axis=1,
        )
        here = rank_ref[b : b + 1, :] == slot
        rows = []
        for x in (offset_ref[b : b + 1, :].astype(F32), value_ref[b : b + 1, :], error_ref[b : b + 1, :]):
            rest = x
            for _ in range(3):
                part = rest.astype(BF16).astype(F32)
                rows.append(jnp.where(here, part, 0.0).astype(BF16))
                rest = rest - part
        t = lax.dot_general(
            jnp.concatenate(rows, axis=0), hot, (((1,), (1,)), ((), ())), preferred_element_type=F32
        )
        for f in range(3):
            at = f * 24
            even, odd = by_parity((t[at : at + 8] + t[at + 8 : at + 16]) + t[at + 16 : at + 24])
            same = jnp.where(odd_device, odd, even)
            other = jnp.where(odd_device, even, odd)
            field_ref[(b * 3 + f) * 8 : (b * 3 + f) * 8 + 8, :] = jnp.concatenate([same, other], axis=0)


def columns(row):
    return jnp.broadcast_to(row, (LANES, LANES)).T


def stats(raw, value, error):
    mean = jnp.sum(raw, axis=0, keepdims=True) * (1.0 / MEMBERS)
    anom = raw - mean
    varian = jnp.sum(anom * anom, axis=0, keepdims=True) * (1.0 / (MEMBERS - 1)) + 1e-06
    total = varian + error
    shrink = jnp.sqrt(error / total)
    scale = -1.0 / ((MEMBERS - 1) * total * (1.0 + shrink))
    push = anom - (value - mean) * (1.0 + shrink)
    return anom, anom * scale, push


def owner_weights(me_ref, table_ref):
    table8 = jnp.broadcast_to(table_ref[...], (8, LANES))
    par = me_ref[0] % 2
    delta = me_ref[0] // 2 - iota((8, LANES), 1) % 64
    steps = jnp.abs(delta)
    far = jnp.take_along_axis(table8, steps, axis=1)[0:1]
    near = jnp.take_along_axis(table8, jnp.maximum(steps - 1, 0), axis=1)[0:1]
    other = jnp.take_along_axis(table8, jnp.abs(2 * delta + 2 * par - 1) // 2, axis=1)[0:1]
    ahead = delta[0:1] > 0
    return jnp.where(ahead, near, far), jnp.where(ahead, far, near), jnp.where(ahead, 0.0, 1.0), other


def field(field_ref, b, f, lo, hi):
    base = (b * 3 + f) * 8
    return jnp.concatenate([field_ref[base + i : base + i + 1, :] for i in range(lo, hi)], axis=1)


def obs_columns(ref, stride, first, b):
    return jnp.concatenate(
        [
            jnp.concatenate(
                [ref[pl.ds(first + r * 8 + b * 4 + s, NDEV, stride=stride), :] for r in range(2)], axis=0
            )
            for s in range(4)
        ],
        axis=1,
    )


def state_columns(recv_ref, at):
    return jnp.concatenate(
        [
            jnp.concatenate(
                [recv_ref[pl.ds((at + h) * 2 + r, NDEV, stride=MSG), :] for r in range(2)], axis=0
            )
            for h in range(WIDE // LANES)
        ],
        axis=1,
    )


def same_gain(cov, at, thr, low, high):
    pieces = []
    for k in range(4):
        line = []
        for h in range(WIDE // LANES):
            c = cov[k * LANES : (k + 1) * LANES, h * LANES : (h + 1) * LANES]
            place = (iota((LANES, LANES), 1) + (at + h) * LANES).astype(F32)
            line.append(c * jnp.where(place >= thr[k * LANES : (k + 1) * LANES, :], high, low))
        pieces.append(jnp.concatenate(line, axis=1))
    return split(jnp.concatenate(pieces, axis=0))


def first_kernel(
    me_ref, table_ref, field_ref, recv_ref, new_ref, left_hi, left_lo, push_hi, push_lo, low, high, thr
):
    w_low, w_high, shift, _ = owner_weights(me_ref, table_ref)
    low[...] = columns(w_low)
    high[...] = columns(w_high)
    _, scaled, push = stats(
        obs_columns(recv_ref, MSG, STATE_ROWS, 0), field(field_ref, 0, 1, 0, 4), field(field_ref, 0, 2, 0, 4)
    )
    left_hi[...], left_lo[...] = split(scaled.T)
    push_hi[...], push_lo[...] = split(push)
    off = field(field_ref, 0, 0, 0, 4)
    for s in range(4):
        thr[s * LANES : (s + 1) * LANES, :] = columns(off[:, s * LANES : (s + 1) * LANES] + shift)

    for t in range(NV_DEV // WIDE):
        at = t * (WIDE // LANES)
        raw = state_columns(recv_ref, at)
        cov = dot3((left_hi[...], left_lo[...]), split(raw))
        gain = same_gain(cov, at, thr, low[...], high[...])
        raw = raw + dot3((push_hi[...], push_lo[...]), gain)
        new_ref[:, t * WIDE : (t + 1) * WIDE] = raw


def main_kernel(
    me_ref, table_ref, field_ref, recv_ref, other_ref, new_ref,
    first_left_hi, first_left_lo, first_push_hi, first_push_lo, low, high, out_ref,
    left_hi, left_lo, push_hi, push_lo, left2_hi, left2_lo, push2_hi, push2_lo, const_hi, const_lo, thr,
):
    par = me_ref[0] % 2
    table = jnp.broadcast_to(table_ref[...], (LANES, LANES))
    _, _, shift, w_other = owner_weights(me_ref, table_ref)
    w_other4 = jnp.concatenate([w_other] * 4, axis=1)

    def set_const(b, scaled, push):
        const = dot3(push, split(scaled * w_other4), BOTH_LANES)
        const_hi[b, :, :], const_lo[b, :, :] = split(const)

    off1 = field(field_ref, 0, 0, 0, 8)
    off2 = field(field_ref, 1, 0, 0, 8)
    d = iota((LANES, LANES), 1) % 64 - iota((LANES, LANES), 0) % 64
    ad = jnp.abs(d)
    far = jnp.take_along_axis(table, ad, axis=1)
    near = jnp.take_along_axis(table, jnp.maximum(ad - 1, 0), axis=1)
    sign = jnp.where(d > 0, 1.0, jnp.where(d < 0, -1.0, 0.0))
    to_same = jnp.take_along_axis(table, jnp.abs(2 * d + 2 * par - 1) // 2, axis=1)
    to_other = jnp.take_along_axis(table, jnp.abs(2 * d + 1 - 2 * par) // 2, axis=1)

    def alike(cov, first):
        pieces = []
        for k in range(4):
            at = first + k * LANES
            column = columns(off1[:, at : at + LANES])
            line = []
            for h in range(4):
                gap = off2[:, first + h * LANES : first + (h + 1) * LANES] - column
                c = cov[k * LANES : (k + 1) * LANES, h * LANES : (h + 1) * LANES]
                line.append(c * jnp.where(gap * sign >= 0.0, far, near))
            pieces.append(jnp.concatenate(line, axis=1))
        return jnp.concatenate(pieces, axis=0)

    def unlike(cov, weight):
        return cov * jnp.concatenate([jnp.concatenate([weight] * 4, axis=1)] * 4, axis=0)

    same2 = obs_columns(recv_ref, MSG, STATE_ROWS, 1)
    other2 = obs_columns(other_ref, OBS_ROWS, 0, 1)
    same2_parts = split(same2)
    other2_parts = split(other2)
    left_same = (first_left_hi[...], first_left_lo[...])
    cov_same = dot3(left_same, same2_parts)
    _, scaled, push = stats(
        obs_columns(other_ref, OBS_ROWS, 0, 0), field(field_ref, 0, 1, 4, 8), field(field_ref, 0, 2, 4, 8)
    )
    left_hi[...], left_lo[...] = split(scaled.T)
    push_hi[...], push_lo[...] = split(push)
    left_other = (left_hi[...], left_lo[...])
    cov_other = dot3(left_other, same2_parts)
    push_all = (
        jnp.concatenate([first_push_hi[...], push_hi[...]], axis=1),
        jnp.concatenate([first_push_lo[...], push_lo[...]], axis=1),
    )
    gain = split(jnp.concatenate([alike(cov_same, 0), unlike(cov_other, to_same)], axis=0))
    same2 = same2 + dot3(push_all, gain)
    cov_same = dot3(left_same, other2_parts)
    cov_other = dot3(left_other, other2_parts)
    set_const(0, scaled, (push_hi[...], push_lo[...]))
    _, scaled, push = stats(same2, field(field_ref, 1, 1, 0, 4), field(field_ref, 1, 2, 0, 4))
    left2_hi[...], left2_lo[...] = split(scaled.T)
    push2_hi[...], push2_lo[...] = split(push)
    for s in range(4):
        thr[s * LANES : (s + 1) * LANES, :] = columns(off2[:, s * LANES : (s + 1) * LANES] + shift)
    gain = split(jnp.concatenate([unlike(cov_same, to_other), alike(cov_other, HALF)], axis=0))
    other2 = other2 + dot3(push_all, gain)
    _, scaled, push = stats(other2, field(field_ref, 1, 1, 4, 8), field(field_ref, 1, 2, 4, 8))
    set_const(1, scaled, split(push))

    for t in range(NV_DEV // WIDE):
        at = t * (WIDE // LANES)
        before = split(state_columns(recv_ref, at))
        raw = new_ref[:, t * WIDE : (t + 1) * WIDE]
        raw = raw + dot3((const_hi[0], const_lo[0]), before)
        centred = split(raw)
        cov = dot3((left2_hi[...], left2_lo[...]), centred)
        gain = same_gain(cov, at, thr, low[...], high[...])
        left = (
            jnp.concatenate([push2_hi[...], const_hi[1]], axis=1),
            jnp.concatenate([push2_lo[...], const_lo[1]], axis=1),
        )
        right = tuple(jnp.concatenate([g, c], axis=0) for g, c in zip(gain, centred))
        raw = raw + dot3(left, right)
        for h in range(WIDE // LANES):
            for r in range(2):
                out_ref[pl.ds((at + h) * 2 + r, NDEV, stride=STATE_ROWS), :] = raw[
                    r * NDEV : (r + 1) * NDEV, h * LANES : (h + 1) * LANES
                ]


VMEM = pl.BlockSpec(memory_space=pltpu.VMEM)
SMEM = pl.BlockSpec(memory_space=pltpu.SMEM)
HBM = pl.BlockSpec(memory_space=pltpu.HBM)


def params(mib):
    return pltpu.CompilerParams(vmem_limit_bytes=mib * 1024 * 1024)


def cost(flops, bytes_accessed):
    return pl.CostEstimate(flops=flops, bytes_accessed=bytes_accessed, transcendentals=0)


def in_hbm(x):
    return pltpu.with_memory_space_constraint(x, pltpu.HBM)


def prep(me, owner, offset, state):
    return pl.pallas_call(
        prep_kernel,
        out_shape=(
            jax.ShapeDtypeStruct((NDEV, MSG, LANES), F32),
            jax.ShapeDtypeStruct((2, NOBS), F32),
        ),
        in_specs=[SMEM] + [HBM] * 3,
        out_specs=(VMEM, VMEM),
        scratch_shapes=[
            pltpu.VMEM((2, NOBS), jnp.int32),
            pltpu.VMEM((2, NOBS), jnp.int32),
            pltpu.SemaphoreType.DMA((2,)),
            pltpu.SemaphoreType.DMA((PIECES,)),
        ],
        compiler_params=params(16),
        name="prep",
    )(me, owner, offset, state)


def sort_out(me, owner, offset, value, error, rank, recv):
    return pl.pallas_call(
        field_kernel,
        out_shape=(
            jax.ShapeDtypeStruct((NDEV, OBS_ROWS, LANES), F32),
            jax.ShapeDtypeStruct((48, LANES), F32),
        ),
        in_specs=[SMEM] + [VMEM] * 6,
        out_specs=(VMEM, VMEM),
        compiler_params=params(16),
        name="fields",
    )(me, owner, offset, value, error, rank, recv)


def assimilate_first(me, table, fields, recv):
    return pl.pallas_call(
        first_kernel,
        out_shape=(
            jax.ShapeDtypeStruct((MEMBERS, NV_DEV), F32),
            jax.ShapeDtypeStruct((HALF, MEMBERS), BF16),
            jax.ShapeDtypeStruct((HALF, MEMBERS), BF16),
            jax.ShapeDtypeStruct((MEMBERS, HALF), BF16),
            jax.ShapeDtypeStruct((MEMBERS, HALF), BF16),
            jax.ShapeDtypeStruct((LANES, LANES), F32),
            jax.ShapeDtypeStruct((LANES, LANES), F32),
        ),
        in_specs=[SMEM] + [VMEM] * 3,
        out_specs=(VMEM,) * 7,
        scratch_shapes=[pltpu.VMEM((HALF, LANES), F32)],
        compiler_params=params(VMEM_MIB),
        cost_estimate=cost(3 * 2**31, 5 * 2**20),
        name="first",
    )(me, table, fields, recv)


def assimilate(me, table, fields, recv, other, first):
    return pl.pallas_call(
        main_kernel,
        out_shape=jax.ShapeDtypeStruct((NDEV * STATE_ROWS, LANES), F32),
        in_specs=[SMEM] + [VMEM] * 11,
        out_specs=VMEM,
        scratch_shapes=[
            pltpu.VMEM((HALF, MEMBERS), BF16),
            pltpu.VMEM((HALF, MEMBERS), BF16),
            pltpu.VMEM((MEMBERS, HALF), BF16),
            pltpu.VMEM((MEMBERS, HALF), BF16),
            pltpu.VMEM((HALF, MEMBERS), BF16),
            pltpu.VMEM((HALF, MEMBERS), BF16),
            pltpu.VMEM((MEMBERS, HALF), BF16),
            pltpu.VMEM((MEMBERS, HALF), BF16),
            pltpu.VMEM((2, MEMBERS, MEMBERS), BF16),
            pltpu.VMEM((2, MEMBERS, MEMBERS), BF16),
            pltpu.VMEM((HALF, LANES), F32),
        ],
        compiler_params=params(VMEM_MIB),
        cost_estimate=cost(9 * 2**31, 9 * 2**20),
        name="assimilate",
    )(me, table, fields, recv, other, *first)


def body(prior_state, obs_value, obs_error, obs_owner, obs_offset, taper_table):
    axes = ("mem", "var")
    me = lax.axis_index(axes).astype(jnp.int32).reshape(1)
    state = prior_state.reshape(2, NDEV * TILES, LANES).transpose(1, 0, 2).reshape(NDEV, STATE_ROWS, LANES)
    msg, rank = prep(me, in_hbm(obs_owner), in_hbm(obs_offset), in_hbm(state))
    recv = lax.all_to_all(msg, axes, split_axis=0, concat_axis=0, tiled=True)
    table = jnp.pad(taper_table, (0, LANES - taper_table.shape[0])).reshape(1, LANES)
    mine, fields = sort_out(me, obs_owner, obs_offset, obs_value, obs_error, rank, recv)
    other = lax.ppermute(mine, axes, [(i, i ^ 1) for i in range(NDEV)]).reshape(NDEV * OBS_ROWS, LANES)
    recv = recv.reshape(NDEV * MSG, LANES)
    first = assimilate_first(me, table, fields, recv)
    new = assimilate(me, table, fields, recv, other, first)
    back = lax.all_to_all(
        new.reshape(NDEV, STATE_ROWS, LANES), axes, split_axis=0, concat_axis=0, tiled=True
    )
    rows = back.reshape(NDEV * TILES, 2, LANES).transpose(1, 0, 2)
    rows = with_layout_constraint(rows, Layout(major_to_minor=(1, 0, 2)))
    return rows.reshape(2, NDEV * NV_DEV)


def solution(mesh):
    in_specs = (P(("mem", "var"), None), P(), P(), P(), P(), P())
    out_specs = P(("mem", "var"), None)
    return jax.shard_map(body, mesh=mesh, in_specs=in_specs, out_specs=out_specs, check_vma=False)
```
